512 devices in a mesh: grp: 16 (over x_hi, z), sp: 32 (over y, x_lo, core).
Axes of the slice: x: 4 (x_hi: 2, x_lo: 2; x = x_hi * 2 + x_lo), y: 8, z: 8, core: 2. Of those that a mesh axis runs over, the one named last changes fastest.
Arguments:
- residual_in: bfloat16 [16, 32, 24, 3072], P('grp', 'sp'), may hold values from -36 to 36
- cached: bfloat16 [2, 16, 32, 24, 3072], P(None, 'grp', 'sp'), may hold values from -3 to 3
- use_cached: int32 [2, 16, 32, 24], P(None, 'grp', 'sp'), may hold values 0 or 1
- queries: bfloat16 [16, 32, 24, 2048], P('grp', 'sp'), may hold values from -6.8 to 6.8
- attn_keys: bfloat16 [16, 32, 24, 2048], P('grp', 'sp'), may hold values from -6.8 to 6.8
- values: bfloat16 [16, 32, 24, 2048], P('grp', 'sp'), may hold values from -6 to 6
- gate_mod: float32 [3072], replicated, may hold values from 1 to 4
- shift_mod: float32 [3072], replicated, may hold values from -3 to 3
- scale_mod: float32 [3072], replicated, may hold values from -0.5 to 0.5
- out_weight: bfloat16 [2048, 3072], P('grp'), may hold values from -0.125 to 0.125
- final_weight: bfloat16 [3072, 64], replicated, may hold values from -0.109375 to 0.109375
- final_bias: float32 [64], replicated, may hold values from -2 to 2
- first_weight: bfloat16 [3, 3, 3, 16, 512], replicated, may hold values from -0.3125 to 0.3125
- first_bias: float32 [512], replicated, may hold values from -2 to 2
- second_weight: bfloat16 [512, 3, 3, 3, 512], P('sp'), may hold values from -0.0546875 to 0.0546875
Outputs:
- stream: bfloat16 [16, 32, 24, 3072], P('grp', 'sp')
- decoded: bfloat16 [512, 48, 1024], P('sp', 'grp')
The draws below stay inside these ranges and needn't reach their ends.
All inputs are finite; a program needn't handle non-finite values. No bound on the sum of `use_cached` on one device may be relied on, other than what follows from the above.
Results may differ from the reference program's by a relative error of at most 0.02.
Values may be sent and summed in bfloat16 or wider, within the bound.
No kernel may reach another device: no remote copies, remote signals or barrier semaphores. Data moves between devices by JAX's collectives and lax.ppermute only.
A program may use at most 128 MiB of HBM per device.

```python
import math
import jax
import jax.numpy as jnp
from jax import lax

D = 3072
HD = 128
CH = 512
LAT = 16
HEADS = 16
CACHE = 2
PH = 24
FR = 16
PW = 32
LH = 48
LW = 64
N_GRP = 16


def draw_residual_in(key, part):
    noise_key, row_key, col_key = jax.random.split(key, 3)
    shape_all = (FR, PW, PH, D)
    row_scale = jnp.exp(jax.random.uniform(row_key, (FR, PW, PH, 1), jnp.float32, math.log(0.3), math.log(3.0)))
    col_scale = jnp.exp(jax.random.uniform(col_key, (D,), jnp.float32, math.log(0.3), math.log(3.0)))
    noise_part = jnp.clip(jax.random.normal(noise_key, shape_all, jnp.float32), -4.0, 4.0)
    return (noise_part * row_scale * col_scale).astype(jnp.bfloat16)


def drawn(key, which):
    seq_total = FR * PW * PH
    width_all = HEADS * HD
    noise_key = jax.random.fold_in(key, which)
    noise_part = jnp.clip(1.7 * jax.random.normal(noise_key, (seq_total, width_all), jnp.float32), -6.75, 6.75)
    return noise_part.reshape(FR, PW, PH, width_all).astype(jnp.bfloat16)


def draw_queries(key, part):
    return drawn(key, 1)


def draw_attn_keys(key, part):
    return drawn(key, 2)


def plant(drawn, key, least, high):
    extent = drawn.shape
    spot = [jax.random.randint(jax.random.fold_in(key, axis), (), 0, extent[axis]) for axis in range(len(extent))]
    drawn = drawn.at[tuple(spot)].set(least)
    longest = extent.index(max(extent))
    spot[longest] = (spot[longest] + 1) % extent[longest]
    return drawn.at[tuple(spot)].set(high)


def block_levels(own_key, extent, cuts, smallest, top_value):
    gain = 1.0
    for dim, blocks in cuts:
        draws = jax.random.uniform(jax.random.fold_in(jax.random.fold_in(own_key, 6), dim), (blocks,), jnp.float32, smallest / len(cuts), top_value / len(cuts))
        gain = gain * jnp.repeat(jnp.exp(draws), extent[dim] // blocks).reshape((-1,) + (1,) * (len(extent) - 1 - dim))
    return gain


def gaussian(key, extent, scale, limit, pieces=(), kind=jnp.bfloat16):
    result = scale * jax.random.normal(key, extent, jnp.float32)
    if pieces:
        result = result * block_levels(key, extent, pieces, -0.22, 0.18)
    return jnp.clip(result, -limit, limit).astype(kind)


def setup_inputs(seed: int = 0) -> dict:
    key_list = jax.random.split(jax.random.key(seed), 16)
    residual_in = draw_residual_in(jax.random.fold_in(key_list[15], 71), 0)
    cached = gaussian(key_list[1], (CACHE, FR, PW, PH, D), 0.5, 3.0, ((1, 16), (2, 32)))
    use_cached = plant((jax.random.randint(key_list[2], (CACHE, FR, PW, PH), 0, 2) < 1).astype(jnp.int32), jax.random.fold_in(key_list[2], 1), 0, 1)
    queries = draw_queries(jax.random.fold_in(key_list[15], 71), 0)
    attn_keys = draw_attn_keys(jax.random.fold_in(key_list[15], 71), 0)
    values = gaussian(key_list[5], (FR, PW, PH, HEADS * HD), 1.0, 6.0, ((0, 16), (1, 32)))
    gate_mod = jnp.clip(jnp.exp(jax.random.uniform(key_list[6], (D,), jnp.float32, math.log(1.0), math.log(4.0))), 1.0, 4.0)
    shift_mod = gaussian(key_list[7], (D,), 0.5, 3.0, (), jnp.float32)
    scale_mod = jnp.clip(jax.random.uniform(key_list[8], (D,), jnp.float32, -0.5, 0.5), -0.5, 0.5)
    out_weight = gaussian(key_list[9], (HEADS * HD, D), (HEADS * HD) ** -0.5, 0.125, ((0, 16),))
    final_weight = gaussian(key_list[10], (D, 4 * LAT), D ** -0.5, 0.109375)
    final_bias = gaussian(key_list[11], (4 * LAT,), 0.3, 2.0, (), jnp.float32)
    first_weight = gaussian(key_list[12], (3, 3, 3, LAT, CH), (27 * LAT) ** -0.5, 0.3125)
    first_bias = gaussian(key_list[13], (CH,), 0.3, 2.0, (), jnp.float32)
    second_weight = gaussian(key_list[14], (CH, 3, 3, 3, CH), (27 * CH) ** -0.5, 0.0546875, ((0, 32),))
    return dict(residual_in=residual_in, cached=cached, use_cached=use_cached, queries=queries, attn_keys=attn_keys, values=values, gate_mod=gate_mod, shift_mod=shift_mod, scale_mod=scale_mod, out_weight=out_weight, final_weight=final_weight, final_bias=final_bias, first_weight=first_weight, first_bias=first_bias, second_weight=second_weight)


def head_attention(query_head, key_head, value_head):
    seq_total = query_head.shape[0]
    head_width = query_head.shape[1]
    block_rows = math.gcd(seq_total, 1024)
    factor = 1.0 / math.sqrt(head_width)
    query_blocks = query_head.reshape(seq_total // block_rows, block_rows, head_width)

    def one_block(query_matrix_rows):
        scores = jnp.dot(query_matrix_rows, key_head.T, preferred_element_type=jnp.float32) * factor
        weights_now = jnp.exp(scores - lax.optimization_barrier(jnp.max(scores, axis=1, keepdims=True)))
        totals = lax.optimization_barrier(jnp.sum(weights_now, axis=1, keepdims=True))
        summed_total = jnp.dot(weights_now.astype(jnp.bfloat16), value_head, preferred_element_type=jnp.float32)
        return (summed_total / totals).astype(jnp.bfloat16)
    return lax.map(one_block, query_blocks).reshape(seq_total, head_width)

def attend_heads(triple):
    return head_attention(triple[0], triple[1], triple[2])

def causal_pad(volume):
    padded = jnp.concatenate([volume[:1], volume[:1], volume], axis=0)
    return jnp.pad(padded, ((0, 0), (1, 1), (1, 1), (0, 0)))

def reference(residual_in, cached, use_cached, queries, attn_keys, values, gate_mod, shift_mod, scale_mod, out_weight, final_weight, final_bias, first_weight, first_bias, second_weight):
    seq_total = FR * PW * PH
    mixed = residual_in.astype(jnp.float32)
    for index_b in range(CACHE):
        mixed = mixed + use_cached[index_b].astype(jnp.float32)[..., None] * cached[index_b].astype(jnp.float32)
    mixed = mixed.reshape(seq_total, D)
    query_heads = jnp.transpose(queries.reshape(seq_total, HEADS, HD), (1, 0, 2))
    key_heads = jnp.transpose(attn_keys.reshape(seq_total, HEADS, HD), (1, 0, 2))
    value_heads = jnp.transpose(values.reshape(seq_total, HEADS, HD), (1, 0, 2))
    attended = lax.map(attend_heads, (query_heads, key_heads, value_heads))
    attended = jnp.transpose(attended, (1, 0, 2)).reshape(seq_total, HEADS * HD)
    group_width = HEADS * HD // N_GRP
    projected_output = jnp.zeros((seq_total, D), jnp.float32)
    for group in range(N_GRP):
        lower = group * group_width
        partial_sum = jnp.dot(attended[:, lower:lower + group_width], out_weight[lower:lower + group_width], preferred_element_type=jnp.float32)
        rounded_result = lax.optimization_barrier(partial_sum.astype(jnp.bfloat16))
        projected_output = projected_output + rounded_result.astype(jnp.float32)
    stream = (mixed + gate_mod.astype(jnp.float32)[None, :] * projected_output).astype(jnp.bfloat16)
    normed_in = stream.astype(jnp.float32)
    center = lax.optimization_barrier(jnp.mean(normed_in, axis=1, keepdims=True))
    spread = lax.optimization_barrier(jnp.mean(jnp.square(normed_in - center), axis=1, keepdims=True))
    modulated = ((normed_in - center) * lax.rsqrt(spread + 1e-06) * (1.0 + scale_mod.astype(jnp.float32))[None, :] + shift_mod.astype(jnp.float32)[None, :]).astype(jnp.bfloat16)
    latent_tokens = (jnp.dot(modulated, final_weight, preferred_element_type=jnp.float32) + final_bias.astype(jnp.float32)[None, :]).astype(jnp.bfloat16)
    split_tokens = latent_tokens.reshape(FR, PW, PH, 2, 2, LAT)
    latent = jnp.transpose(split_tokens, (0, 2, 3, 1, 4, 5)).reshape(FR, LH, LW, LAT)
    latent_pad = causal_pad(latent)
    tap_slices = []
    for time_tap in range(3):
        for row_tap in range(3):
            for col_tap in range(3):
                tap_slices.append(latent_pad[time_tap:time_tap + FR, row_tap:row_tap + LH, col_tap:col_tap + LW])
    patches = jnp.concatenate(tap_slices, axis=3)
    first_out = (jnp.dot(patches, first_weight.reshape(27 * LAT, CH), preferred_element_type=jnp.float32) + first_bias.astype(jnp.float32)).astype(jnp.bfloat16)
    activated = jax.nn.silu(first_out.astype(jnp.float32)).astype(jnp.bfloat16)
    act_pad = causal_pad(activated)
    summed_total = jnp.zeros((FR, LH, LW, CH), jnp.float32)
    for time_tap in range(3):
        for row_tap in range(3):
            for col_tap in range(3):
                tap_input = act_pad[time_tap:time_tap + FR, row_tap:row_tap + LH, col_tap:col_tap + LW]
                summed_total = summed_total + lax.dot_general(tap_input, second_weight[:, time_tap, row_tap, col_tap, :], (((3,), (1,)), ((), ())), preferred_element_type=jnp.float32)
    cells = (summed_total + first_out.astype(jnp.float32)).astype(jnp.bfloat16)
    decoded = jnp.transpose(cells, (3, 1, 0, 2)).reshape(CH, LH, FR * LW)
    return (stream.reshape(FR, PW, PH, D), decoded)
```

```python
import math

import jax
import jax.numpy as jnp
from jax import lax
from jax.experimental import pallas as pl
from jax.experimental.pallas import tpu as pltpu
from jax.sharding import Mesh, PartitionSpec as P

HD = 128
HEADS = 16
F32 = jnp.float32
BF16 = jnp.bfloat16
MIB = 1 << 20

TOK = 24
FRAMES = 16
PIX = 1024
SUB = 128

VMEM = pl.BlockSpec(memory_space=pltpu.VMEM)
SMEM = pl.BlockSpec(memory_space=pltpu.SMEM)

GRP = ("h", "z")
COL = ("ya", "yb", "l", "c")


def dot(a, b, contract):
    return lax.dot_general(a, b, ((contract[0], contract[1]), ((), ())), preferred_element_type=F32)


def pack_kernel(q_ref, k_ref, v_ref, out_ref):
    for g in range(HEADS):
        cols = slice(g * HD, (g + 1) * HD)
        out_ref[g, :, 0:HD] = q_ref[:, cols]
        out_ref[g, :, HD : 2 * HD] = k_ref[:, cols]
        out_ref[g, :, 2 * HD : 3 * HD] = v_ref[:, cols]


def pack(q, k, v):
    return pl.pallas_call(
        pack_kernel,
        out_shape=jax.ShapeDtypeStruct((HEADS, TOK, 3 * HD), BF16),
        in_specs=[VMEM] * 3,
        out_specs=VMEM,
    )(q, k, v)


def attend_kernel(q_ref, kv_ref, out_ref):
    scale = math.log2(math.e) / math.sqrt(HD)
    rows = q_ref.shape[1]
    keys = kv_ref[:, 0:HD]
    vals = kv_ref[:, HD : 2 * HD]
    outs, logs = [], []
    for i in range(rows // SUB):
        q = q_ref[0, i * SUB : (i + 1) * SUB, :]
        s = dot(q, keys, ((1,), (1,)))
        top = jnp.max(s, axis=1, keepdims=True)
        p = jnp.exp2(s * scale - top * scale)
        total = jnp.sum(p, axis=1, keepdims=True)
        o = dot(p.astype(BF16), vals, ((1,), (0,)))
        outs.append(o / total)
        logs.append(top * scale + jnp.log2(total))
    o = jnp.concatenate(outs, axis=0).reshape(2, 8, TOK, HD)
    log = jnp.concatenate(logs, axis=0)
    hi = log.astype(BF16).astype(F32)
    mid = (log - hi).astype(BF16).astype(F32)
    lo = log - hi - mid
    hi, mid, lo = (x.reshape(2, 8, TOK, 1) for x in (hi, mid, lo))
    token = lax.broadcasted_iota(jnp.int32, (2 * TOK, HD), 0)
    lane = lax.broadcasted_iota(jnp.int32, (2 * TOK, HD), 1)
    base = lane - lax.rem(token, 3) * 3
    row = lax.broadcasted_iota(jnp.int32, (16, 2 * TOK), 0)
    spot = lax.broadcasted_iota(jnp.int32, (16, 2 * TOK), 1)
    pick = jnp.where(lax.div(spot, 3) == row, 1.0, 0.0).astype(BF16)
    for z in range(8):
        piece = [jnp.concatenate([x[0, z], x[1, z]], axis=0) for x in (hi, mid, lo)]
        spread = jnp.where(
            base == 0,
            piece[0],
            jnp.where(base == 1, piece[1], jnp.where(base == 2, piece[2], 0.0)),
        )
        stats = dot(pick, spread.astype(BF16), ((1,), (0,)))
        out_ref[z, 0] = jnp.concatenate([o[0, z], o[1, z], stats], axis=0).astype(BF16)


def attend(q, kv):
    return pl.pallas_call(
        attend_kernel,
        grid=(4,),
        out_shape=jax.ShapeDtypeStruct((8, 4, 64, HD), BF16),
        in_specs=[
            pl.BlockSpec((1, FRAMES * TOK, HD), lambda i: (i, 0, 0)),
            pl.BlockSpec(kv.shape, lambda i: (0, 0)),
        ],
        out_specs=pl.BlockSpec((8, 1, 64, HD), lambda i: (0, i, 0, 0)),
        compiler_params=pltpu.CompilerParams(vmem_limit_bytes=48 * MIB),
    )(q, kv)


def project_kernel(h_ref, parts_ref, weight_ref, keep_ref, send_ref, att_ref, sum_ref):
    @pl.when(pl.program_id(0) == 0)
    def join():
        token = lax.broadcasted_iota(jnp.int32, (2 * TOK, HD), 0)
        lane = lax.broadcasted_iota(jnp.int32, (2 * TOK, HD), 1)
        base = lane - lax.rem(token, 3) * 3
        mine = (base >= 0) & (base < 3)
        spot = lax.broadcasted_iota(jnp.int32, (2 * TOK, 16), 0)
        row = lax.broadcasted_iota(jnp.int32, (2 * TOK, 16), 1)
        pick = jnp.where(lax.div(spot, 3) == row, 1.0, 0.0).astype(BF16)
        for z in range(8):
            logs = []
            for j in range(4):
                spread = dot(pick, parts_ref[z, j, 48:64, :], ((1,), (0,)))
                logs.append(jnp.sum(jnp.where(mine, spread, 0.0), axis=1, keepdims=True))
            top = jnp.maximum(jnp.maximum(logs[0], logs[1]), jnp.maximum(logs[2], logs[3]))
            shares = [jnp.exp2(x - top) for x in logs]
            total = (shares[0] + shares[1]) + (shares[2] + shares[3])
            att = jnp.zeros((2 * TOK, HD), F32)
            for j in range(4):
                att = att + parts_ref[z, j, 0:48, :].astype(F32) * (shares[j] / total)
            att_ref[:, z * HD : (z + 1) * HD] = att.astype(BF16)

    sum_ref[...] = dot(att_ref[...], weight_ref[...], ((1,), (0,)))
    h = h_ref[0]
    keep_ref[...] = sum_ref[pl.ds(pl.multiple_of(h * TOK, 8), TOK), :]
    send_ref[...] = sum_ref[pl.ds(pl.multiple_of((1 - h) * TOK, 8), TOK), :].astype(BF16)


def project(h, parts, weight):
    depth, width = weight.shape
    block = 768
    return pl.pallas_call(
        project_kernel,
        grid=(width // block,),
        out_shape=(
            jax.ShapeDtypeStruct((TOK, width), F32),
            jax.ShapeDtypeStruct((TOK, width), BF16),
        ),
        in_specs=[
            SMEM,
            pl.BlockSpec(parts.shape, lambda i: (0, 0, 0, 0)),
            pl.BlockSpec((depth, block), lambda i: (0, i)),
        ],
        out_specs=(
            pl.BlockSpec((TOK, block), lambda i: (0, i)),
            pl.BlockSpec((TOK, block), lambda i: (0, i)),
        ),
        scratch_shapes=[pltpu.VMEM((2 * TOK, depth), BF16), pltpu.VMEM((2 * TOK, block), F32)],
        compiler_params=pltpu.CompilerParams(vmem_limit_bytes=32 * MIB),
    )(h, parts, weight)


def norm_kernel(
    keep_ref, recv_ref, res_ref, cached_ref, use_ref, gate_ref, shift_ref, scale_ref, fw_ref, fb_ref,
    stream_ref, out_ref,
):
    eye = lax.broadcasted_iota(jnp.int32, (TOK, TOK), 0) == lax.broadcasted_iota(
        jnp.int32, (TOK, TOK), 1
    )
    mixed = res_ref[...].astype(F32)
    for b in range(2):
        used = use_ref[b : b + 1, :].astype(F32)
        column = jnp.sum(jnp.where(eye, used, 0.0), axis=1, keepdims=True)
        mixed = mixed + column * cached_ref[b].astype(F32)
    projected = keep_ref[...] + recv_ref[...].astype(F32)
    stream = (mixed + gate_ref[...] * projected).astype(BF16)
    stream_ref[...] = stream
    x = stream.astype(F32)
    center = jnp.mean(x, axis=1, keepdims=True)
    off = x - center
    spread = jnp.mean(off * off, axis=1, keepdims=True)
    modulated = off * lax.rsqrt(spread + 1e-6) * (1.0 + scale_ref[...]) + shift_ref[...]
    latent = dot(modulated.astype(BF16), fw_ref[...], ((1,), (0,))) + fb_ref[...]
    latent = latent.astype(BF16)
    band = lax.broadcasted_iota(jnp.int32, (FRAMES, TOK), 0)
    source = lax.broadcasted_iota(jnp.int32, (FRAMES, TOK), 1)
    first = lax.div(3 * band, 2) - 1
    pieces = [
        dot(jnp.where(source == first + k, 1.0, 0.0).astype(BF16), latent, ((1,), (0,)))
        for k in range(4)
    ]
    window = jnp.concatenate(pieces, axis=1)
    out_ref[...] = jnp.broadcast_to(window[:, None, :], (FRAMES, 32, 256)).astype(BF16)


def norm(keep, recv, res, cached, use, gate, shift, scale, fw, fb):
    return pl.pallas_call(
        norm_kernel,
        out_shape=(
            jax.ShapeDtypeStruct(res.shape, BF16),
            jax.ShapeDtypeStruct((FRAMES, 32, 256), BF16),
        ),
        in_specs=[VMEM] * 10,
        out_specs=(VMEM, VMEM),
        compiler_params=pltpu.CompilerParams(vmem_limit_bytes=32 * MIB),
    )(keep, recv, res, cached, use, gate, shift, scale, fw, fb)


def frames_back(x, count, lane):
    if count == 0:
        return x
    moved = pltpu.roll(x, 64 * count, 1)
    start = x[:, 0:128]
    start = jnp.where(lane[:, 0:128] < 64, start, pltpu.roll(start, 64, 1))
    width = 128
    head = jnp.where(lane[:, 0:width] < 64 * count, start, moved[:, 0:width])
    return jnp.concatenate([head, moved[:, width:]], axis=1)


def column_shift(x, by, place):
    if by == 0:
        return x
    moved = pltpu.roll(x, (-by) % PIX, 1)
    edge = 63 if by == 1 else 0
    return jnp.where(place == edge, 0.0, moved)


def conv_kernel(place_ref, lat_ref, w1_ref, b1_ref, w2_ref, out_ref, taps_ref, w1t_ref, first_ref, acc_ref):
    band = place_ref[0]
    lanes = place_ref[1]
    w1t_ref[...] = jnp.transpose(w1_ref[...].astype(F32)).astype(BF16)
    flat = jnp.transpose(lat_ref[...].astype(F32))
    lane16 = lax.broadcasted_iota(jnp.int32, (16, PIX), 1)
    place16 = lax.rem(lane16, 64)
    source = lax.broadcasted_iota(jnp.int32, (128, 128), 0)
    target = lax.broadcasted_iota(jnp.int32, (128, 128), 1)
    wanted = (
        lax.rem(target, 2) * 64 + lax.div(target, 64) * 32 + lax.div(lax.rem(target, 64), 2)
    )
    weave = jnp.where(source == wanted, 1.0, 0.0).astype(BF16)
    rows_b = [
        jnp.concatenate([flat[r * 32 + b * 16 : r * 32 + b * 16 + 16] for r in range(8)], axis=0)
        for b in range(2)
    ]
    blocks = []
    for n in range(8):
        both = jnp.concatenate([x[:, n * 64 : (n + 1) * 64] for x in rows_b], axis=1)
        blocks.append(dot(both.astype(BF16), weave, ((1,), (0,))))
    latent = jnp.concatenate(blocks, axis=1)
    for r in range(8):
        row = latent[r * 16 : r * 16 + 16]
        for b in range(3):
            moved = column_shift(row, b - 1, place16)
            for t in range(3):
                at = r * 48 + b * 16
                taps_ref[t, at : at + 16, :] = frames_back(moved, 2 - t, lane16).astype(BF16)
    acc_ref[...] = jnp.zeros_like(acc_ref)
    odd = lax.rem(band, 2)
    bias = b1_ref[...]
    for r in range(5):
        at = pl.multiple_of((odd + r) * 48, 16)
        patches = jnp.concatenate([taps_ref[t, pl.ds(at, 144), :] for t in range(3)], axis=0)
        first = dot(w1t_ref[...], patches, ((1,), (0,))) + bias
        height = 3 * band - 1 + r
        inside = jnp.where((height >= 0) & (height < 48), 1.0, 0.0)
        v = (first * inside).astype(BF16).astype(F32)
        if 1 <= r <= 3:
            first_ref[...] = v
            own = first_ref[pl.ds(pl.multiple_of(lanes * 16, 16), 16), :]
            acc_ref[r - 1, 2, 16:32, :] += own
        half = 0.5 * v
        act = (half * jnp.tanh(half) + half).astype(BF16)
        z = dot(w2_ref[...], act, ((1,), (0,)))
        for a in range(3):
            o = r - a
            if 0 <= o < 3:
                for t in range(3):
                    acc_ref[o, t] += z[(t * 3 + a) * 48 : (t * 3 + a + 1) * 48]
    for o in range(3):
        total = None
        for t in range(3):
            u = acc_ref[o, t, 16:32, :]
            u = u + column_shift(acc_ref[o, t, 0:16, :], -1, place16)
            u = u + column_shift(acc_ref[o, t, 32:48, :], 1, place16)
            u = frames_back(u, 2 - t, lane16)
            total = u if total is None else total + u
        out_ref[o] = total.astype(BF16)


def conv(place, lat, w1, b1, w2):
    return pl.pallas_call(
        conv_kernel,
        out_shape=jax.ShapeDtypeStruct((3, 16, PIX), BF16),
        in_specs=[SMEM] + [VMEM] * 4,
        out_specs=VMEM,
        scratch_shapes=[
            pltpu.VMEM((3, 8 * 48, PIX), BF16),
            pltpu.VMEM((512, 432), BF16),
            pltpu.VMEM((512, PIX), F32),
            pltpu.VMEM((3, 3, 48, PIX), F32),
        ],
        compiler_params=pltpu.CompilerParams(vmem_limit_bytes=56 * MIB),
    )(place, lat, w1, b1, w2)


def per_device(
    residual_in,
    cached,
    use_cached,
    queries,
    attn_keys,
    values,
    gate_mod,
    shift_mod,
    scale_mod,
    out_weight,
    final_weight,
    final_bias,
    first_weight,
    first_bias,
    second_weight,
):
    model_width = residual_in.shape[-1]
    channels = first_weight.shape[-1]
    weight = lax.all_gather(out_weight, "z", axis=0, tiled=True)

    packed = pack(*(x.reshape(TOK, HEADS * HD) for x in (queries, attn_keys, values)))
    moved = lax.all_to_all(packed, GRP, split_axis=0, concat_axis=0, tiled=True)
    moved = moved.reshape(FRAMES * TOK, 3 * HD)
    kv = jnp.broadcast_to(moved[None, :, HD:], (8, FRAMES * TOK, 2 * HD))
    kv = lax.all_to_all(kv, ("yb", "l", "c"), split_axis=0, concat_axis=0, tiled=True)
    q = jnp.broadcast_to(moved[None, :, :HD], (4, FRAMES * TOK, HD))
    q = lax.all_to_all(q, "ya", split_axis=0, concat_axis=0, tiled=True)
    parts = attend(q, kv.reshape(8 * FRAMES * TOK, 2 * HD))
    parts = lax.all_to_all(
        parts.reshape(32, 64, HD), ("z", "ya"), split_axis=0, concat_axis=0, tiled=True
    )
    h = lax.axis_index("h").astype(jnp.int32)
    keep, send = project(h.reshape(1), parts.reshape(8, 4, 64, HD), weight)
    recv = lax.ppermute(send, "h", [(0, 1), (1, 0)])
    stream, windows = norm(
        keep,
        recv,
        residual_in.reshape(TOK, model_width),
        cached.reshape(2, TOK, model_width),
        use_cached.reshape(2, TOK),
        gate_mod[None, :],
        shift_mod[None, :],
        scale_mod[None, :],
        final_weight,
        final_bias[None, :],
    )
    lat = lax.all_to_all(
        windows.reshape(512, 256), GRP + COL, split_axis=0, concat_axis=0, tiled=True
    )
    place = jnp.stack([lax.axis_index(GRP), lax.axis_index(COL)]).astype(jnp.int32)
    w2 = jnp.transpose(second_weight, (1, 2, 3, 0, 4)).reshape(27 * 16, channels)
    out = conv(place, lat, first_weight.reshape(27 * 16, channels), first_bias[:, None], w2)
    return stream.reshape(residual_in.shape), jnp.transpose(out, (1, 0, 2))


def solution(mesh):
    fine = Mesh(mesh.devices.reshape(2, 8, 4, 2, 2, 2), GRP + COL)
    return jax.shard_map(
        per_device,
        mesh=fine,
        in_specs=(
            P(GRP, COL, None, None),
            P(None, GRP, COL, None, None),
            P(None, GRP, COL, None),
            P(GRP, COL, None, None),
            P(GRP, COL, None, None),
            P(GRP, COL, None, None),
            P(),
            P(),
            P(),
            P(GRP, None),
            P(),
            P(),
            P(),
            P(),
            P(COL, None, None, None, None),
        ),
        out_specs=(P(GRP, COL, None, None), P(COL, GRP, None)),
        check_vma=False,
    )
```

```python
import math

import jax
import jax.numpy as jnp
from jax import lax
from jax.experimental import pallas as pl
from jax.experimental.pallas import tpu as pltpu
from jax.sharding import Mesh, PartitionSpec as P

HD = 128
HEADS = 16
F32 = jnp.float32
BF16 = jnp.bfloat16
MIB = 1 << 20

TOK = 24
FRAMES = 16
PIX = 1024
KEYS = 768

VMEM = pl.BlockSpec(memory_space=pltpu.VMEM)
SMEM = pl.BlockSpec(memory_space=pltpu.SMEM)

GRP = ("h", "z")
COL = ("ya", "yb", "l", "c")


def dot(a, b, contract):
    return lax.dot_general(a, b, ((contract[0], contract[1]), ((), ())), preferred_element_type=F32)


def pack_kernel(c_ref, q_ref, k_ref, v_ref, weight_ref, out_ref, half_ref):
    half = half_ref.shape[1]
    half_ref[...] = weight_ref[:, pl.ds(pl.multiple_of(c_ref[0] * half, 128), half)]
    for g in range(HEADS):
        cols = slice(g * HD, (g + 1) * HD)
        out_ref[g, :, 0:HD] = q_ref[:, cols]
        out_ref[g, :, HD : 2 * HD] = k_ref[:, cols]
        out_ref[g, :, 2 * HD : 3 * HD] = v_ref[:, cols]


def pack(c, q, k, v, weight):
    return pl.pallas_call(
        pack_kernel,
        out_shape=(
            jax.ShapeDtypeStruct((HEADS, TOK, 3 * HD), BF16),
            jax.ShapeDtypeStruct((weight.shape[0], weight.shape[1] // 2), BF16),
        ),
        in_specs=[SMEM] + [VMEM] * 4,
        out_specs=(VMEM, VMEM),
    )(c, q, k, v, weight)


def attend_kernel(q_ref, kv0_ref, kv1_ref, out_ref):
    scale = math.log2(math.e) / math.sqrt(HD)
    half = kv0_ref.shape[0]
    token = lax.broadcasted_iota(jnp.int32, (2 * TOK, HD), 0)
    lane = lax.broadcasted_iota(jnp.int32, (2 * TOK, HD), 1)
    base = lane - lax.rem(token, 3) * 3
    row = lax.broadcasted_iota(jnp.int32, (16, 2 * TOK), 0)
    spot = lax.broadcasted_iota(jnp.int32, (16, 2 * TOK), 1)
    pick = jnp.where(lax.div(spot, 3) == row, 1.0, 0.0).astype(BF16)
    runs = [(ref, slice(at, at + KEYS)) for ref in (kv0_ref, kv1_ref) for at in range(0, half, KEYS)]

    def column(i, carry):
        q = q_ref[i]

        def scores(n):
            ref, rows = runs[n]
            return dot(q, ref[rows, 0:HD], ((1,), (1,)))

        ahead = scores(0)
        top = total = o = None
        for n, (ref, rows) in enumerate(runs):
            s = ahead
            if n + 1 < len(runs):
                ahead = scores(n + 1)
            high = jnp.max(s, axis=1, keepdims=True) * scale
            if n:
                before = top
                top = jnp.maximum(before, high)
                shrink = jnp.exp2(before - top)
            else:
                top = high
            p = jnp.exp2(s * scale - top)
            here = jnp.sum(p, axis=1, keepdims=True)
            part = dot(p.astype(BF16), ref[rows, HD : 2 * HD], ((1,), (0,)))
            total = total * shrink + here if n else here
            o = o * shrink + part if n else part
        o = (o / total).reshape(2, 8, TOK, HD)
        log = top + jnp.log2(total)
        hi = log.astype(BF16).astype(F32)
        mid = (log - hi).astype(BF16).astype(F32)
        lo = log - hi - mid
        hi, mid, lo = (x.reshape(2, 8, TOK, 1) for x in (hi, mid, lo))
        for z in range(8):
            piece = [jnp.concatenate([x[0, z], x[1, z]], axis=0) for x in (hi, mid, lo)]
            spread = jnp.where(
                base == 0,
                piece[0],
                jnp.where(base == 1, piece[1], jnp.where(base == 2, piece[2], 0.0)),
            )
            stats = dot(pick, spread.astype(BF16), ((1,), (0,)))
            out_ref[z, i] = jnp.concatenate([o[0, z], o[1, z], stats], axis=0).astype(BF16)
        return carry

    lax.fori_loop(0, 4, column, 0)


def attend(q, kvs):
    return pl.pallas_call(
        attend_kernel,
        out_shape=jax.ShapeDtypeStruct((8, 4, 64, HD), BF16),
        in_specs=[VMEM] * 3,
        out_specs=VMEM,
        compiler_params=pltpu.CompilerParams(vmem_limit_bytes=32 * MIB),
    )(q, *kvs)


def hold_kernel(own_ref, out_ref, sem):
    copy = pltpu.make_async_copy(own_ref, out_ref, sem)
    copy.start()
    copy.wait()


def hold(own):
    return pl.pallas_call(
        hold_kernel,
        out_shape=jax.ShapeDtypeStruct(own.shape, BF16),
        in_specs=[pl.BlockSpec(memory_space=pltpu.HBM)],
        out_specs=VMEM,
        scratch_shapes=[pltpu.SemaphoreType.DMA],
        cost_estimate=pl.CostEstimate(flops=0, bytes_accessed=2 * own.size * 2, transcendentals=0),
        compiler_params=pltpu.CompilerParams(vmem_limit_bytes=8 * MIB),
    )(own)


def project_kernel(h_ref, c_ref, parts_ref, own_ref, other_ref, keep_ref, send_ref, att_ref, sum_ref):
    step = pl.program_id(0)

    @pl.when(step == 0)
    def join():
        join_parts(parts_ref, att_ref)

    @pl.when(step < 2)
    def near():
        sum_ref[...] = dot(att_ref[...], own_ref[...], ((1,), (0,)))

    @pl.when(step >= 2)
    def far():
        sum_ref[...] = dot(att_ref[...], other_ref[...], ((1,), (0,)))

    h = h_ref[0]
    keep_ref[...] = sum_ref[pl.ds(pl.multiple_of(h * TOK, 8), TOK), :]
    send_ref[...] = sum_ref[pl.ds(pl.multiple_of((1 - h) * TOK, 8), TOK), :].astype(BF16)


def join_parts(parts_ref, att_ref):
    token = lax.broadcasted_iota(jnp.int32, (2 * TOK, HD), 0)
    lane = lax.broadcasted_iota(jnp.int32, (2 * TOK, HD), 1)
    base = lane - lax.rem(token, 3) * 3
    mine = (base >= 0) & (base < 3)
    spot = lax.broadcasted_iota(jnp.int32, (2 * TOK, 16), 0)
    row = lax.broadcasted_iota(jnp.int32, (2 * TOK, 16), 1)
    pick = jnp.where(lax.div(spot, 3) == row, 1.0, 0.0).astype(BF16)
    for z in range(8):
        logs = []
        for j in range(4):
            spread = dot(pick, parts_ref[z, j, 48:64, :], ((1,), (0,)))
            logs.append(jnp.sum(jnp.where(mine, spread, 0.0), axis=1, keepdims=True))
        top = jnp.maximum(jnp.maximum(logs[0], logs[1]), jnp.maximum(logs[2], logs[3]))
        shares = [jnp.exp2(x - top) for x in logs]
        total = (shares[0] + shares[1]) + (shares[2] + shares[3])
        att = jnp.zeros((2 * TOK, HD), F32)
        for j in range(4):
            att = att + parts_ref[z, j, 0:48, :].astype(F32) * (shares[j] / total)
        att_ref[:, z * HD : (z + 1) * HD] = att.astype(BF16)


def project(h, c, parts, own, other):
    depth, half = own.shape
    block = half // 2

    def place(i, h_ref, c_ref):
        side = jnp.where(i < 2, c_ref[0], 1 - c_ref[0])
        return 0, side * 2 + lax.rem(i, 2)

    return pl.pallas_call(
        project_kernel,
        out_shape=(
            jax.ShapeDtypeStruct((TOK, 2 * half), F32),
            jax.ShapeDtypeStruct((TOK, 2 * half), BF16),
        ),
        grid_spec=pltpu.PrefetchScalarGridSpec(
            num_scalar_prefetch=2,
            grid=(4,),
            in_specs=[
                pl.BlockSpec(parts.shape, lambda i, h_ref, c_ref: (0, 0, 0, 0)),
                pl.BlockSpec((depth, block), lambda i, h_ref, c_ref: (0, jnp.minimum(i, 1))),
                pl.BlockSpec((depth, block), lambda i, h_ref, c_ref: (0, jnp.maximum(i - 2, 0))),
            ],
            out_specs=(pl.BlockSpec((TOK, block), place), pl.BlockSpec((TOK, block), place)),
            scratch_shapes=[
                pltpu.VMEM((2 * TOK, depth), BF16),
                pltpu.VMEM((2 * TOK, block), F32),
            ],
        ),
        compiler_params=pltpu.CompilerParams(vmem_limit_bytes=24 * MIB),
    )(h, c, parts, own, other)


def norm_kernel(
    h_ref, keep_ref, recv_ref, res_ref, cached_ref, use_ref, gate_ref, shift_ref, scale_ref, fw_ref, fb_ref,
    stream_ref, out_ref,
):
    eye = lax.broadcasted_iota(jnp.int32, (TOK, TOK), 0) == lax.broadcasted_iota(
        jnp.int32, (TOK, TOK), 1
    )
    mixed = res_ref[...].astype(F32)
    for b in range(2):
        used = use_ref[b : b + 1, :].astype(F32)
        column = jnp.sum(jnp.where(eye, used, 0.0), axis=1, keepdims=True)
        mixed = mixed + column * cached_ref[b].astype(F32)
    projected = keep_ref[...] + recv_ref[1 - h_ref[0]].astype(F32)
    stream = (mixed + gate_ref[...] * projected).astype(BF16)
    stream_ref[...] = stream
    x = stream.astype(F32)
    center = jnp.mean(x, axis=1, keepdims=True)
    off = x - center
    spread = jnp.mean(off * off, axis=1, keepdims=True)
    modulated = off * lax.rsqrt(spread + 1e-6) * (1.0 + scale_ref[...]) + shift_ref[...]
    latent = dot(modulated.astype(BF16), fw_ref[...], ((1,), (1,))) + fb_ref[...]
    latent = latent.astype(BF16)
    source = lax.broadcasted_iota(jnp.int32, (64, 64), 0)
    target = lax.broadcasted_iota(jnp.int32, (64, 64), 1)
    group = lax.div(target, 16)
    wanted = (lax.rem(group, 2) * 2 + lax.div(group, 2)) * 16 + lax.rem(target, 16)
    latent = dot(latent, jnp.where(source == wanted, 1.0, 0.0).astype(BF16), ((1,), (0,)))
    latent = latent.astype(BF16)
    band = lax.broadcasted_iota(jnp.int32, (FRAMES, TOK), 0)
    source = lax.broadcasted_iota(jnp.int32, (FRAMES, TOK), 1)
    first = lax.div(3 * band, 2) - 1
    pieces = [
        dot(jnp.where(source == first + k, 1.0, 0.0).astype(BF16), latent, ((1,), (0,)))
        for k in range(4)
    ]
    window = [x[:, 0:32] for x in pieces] + [x[:, 32:64] for x in pieces]
    window = jnp.concatenate(window, axis=1).reshape(FRAMES, 1, 2, HD)
    out_ref[...] = jnp.broadcast_to(window, (FRAMES, 32, 2, HD)).astype(BF16)


def norm(h, keep, recv, res, cached, use, gate, shift, scale, fw, fb):
    return pl.pallas_call(
        norm_kernel,
        out_shape=(
            jax.ShapeDtypeStruct(res.shape, BF16),
            jax.ShapeDtypeStruct((FRAMES, 32, 2, HD), BF16),
        ),
        in_specs=[SMEM] + [VMEM] * 10,
        out_specs=(VMEM, VMEM),
        compiler_params=pltpu.CompilerParams(vmem_limit_bytes=32 * MIB),
    )(h, keep, recv, res, cached, use, gate, shift, scale, fw, fb)


def frames_back(x, count, lane):
    if count == 0:
        return x
    moved = pltpu.roll(x, 64 * count, 1)
    start = x[:, 0:128]
    start = jnp.where(lane[:, 0:128] < 64, start, pltpu.roll(start, 64, 1))
    width = 128
    head = jnp.where(lane[:, 0:width] < 64 * count, start, moved[:, 0:width])
    return jnp.concatenate([head, moved[:, width:]], axis=1)


def column_shift(x, by, place):
    if by == 0:
        return x
    moved = pltpu.roll(x, (-by) % PIX, 1)
    edge = 63 if by == 1 else 0
    return jnp.where(place == edge, 0.0, moved)


def ready_kernel(w1_ref, w2_ref, out_ref):
    taps = w2_ref.shape[0]
    out_ref[0:taps, :] = w2_ref[...]
    out_ref[taps:, 0:taps] = jnp.transpose(w1_ref[...].astype(F32)).astype(BF16)


def ready(w1, w2):
    return pl.pallas_call(
        ready_kernel,
        out_shape=jax.ShapeDtypeStruct((432 + 512, 512), BF16),
        in_specs=[VMEM] * 2,
        out_specs=VMEM,
        cost_estimate=pl.CostEstimate(flops=0, bytes_accessed=1 << 23, transcendentals=0),
        compiler_params=pltpu.CompilerParams(vmem_limit_bytes=8 * MIB),
    )(w1, w2)


def conv_kernel(band_ref, own_ref, lat_ref, weights_ref, b1_ref, out_ref, taps_ref, first_ref, acc_ref):
    band = band_ref[0]
    lanes = own_ref[0]
    bias = jnp.transpose(jnp.broadcast_to(b1_ref[...], (8, 512)))[:, 0:1]
    lane16 = lax.broadcasted_iota(jnp.int32, (16, PIX), 1)
    place16 = lax.rem(lane16, 64)
    latent = jnp.transpose(lat_ref[...].astype(F32).reshape(PIX, 128))
    for r in range(8):
        row = latent[r * 16 : r * 16 + 16]
        for b in range(3):
            moved = column_shift(row, b - 1, place16)
            for t in range(3):
                at = r * 48 + b * 16
                taps_ref[t, at : at + 16, :] = frames_back(moved, 2 - t, lane16).astype(BF16)
    acc_ref[...] = jnp.zeros_like(acc_ref)
    odd = lax.rem(band, 2)
    for r in range(5):
        at = pl.multiple_of((odd + r) * 48, 16)
        patches = jnp.concatenate([taps_ref[t, pl.ds(at, 144), :] for t in range(3)], axis=0)
        first = dot(weights_ref[432:, 0:432], patches, ((1,), (0,))) + bias
        height = 3 * band - 1 + r
        inside = jnp.where((height >= 0) & (height < 48), 1.0, 0.0)
        v = (first * inside).astype(BF16).astype(F32)
        if 1 <= r <= 3:
            first_ref[...] = v
            own = first_ref[pl.ds(pl.multiple_of(lanes * 16, 16), 16), :]
            acc_ref[r - 1, 2, 16:32, :] += own
        half = 0.5 * v
        act = (half * jnp.tanh(half) + half).astype(BF16)
        z = dot(weights_ref[0:432, :], act, ((1,), (0,)))
        for a in range(3):
            o = r - a
            if 0 <= o < 3:
                for t in range(3):
                    acc_ref[o, t] += z[(t * 3 + a) * 48 : (t * 3 + a + 1) * 48]
    for o in range(3):
        total = None
        for t in range(3):
            u = acc_ref[o, t, 16:32, :]
            u = u + column_shift(acc_ref[o, t, 0:16, :], -1, place16)
            u = u + column_shift(acc_ref[o, t, 32:48, :], 1, place16)
            u = frames_back(u, 2 - t, lane16)
            total = u if total is None else total + u
        out_ref[o] = total.astype(BF16)


def conv(band, own, lat, weights, b1):
    return pl.pallas_call(
        conv_kernel,
        out_shape=jax.ShapeDtypeStruct((3, 16, PIX), BF16),
        in_specs=[SMEM] * 2 + [VMEM] * 3,
        out_specs=VMEM,
        scratch_shapes=[
            pltpu.VMEM((3, 8 * 48, PIX), BF16),
            pltpu.VMEM((512, PIX), F32),
            pltpu.VMEM((3, 3, 48, PIX), F32),
        ],
        compiler_params=pltpu.CompilerParams(vmem_limit_bytes=28 * MIB),
    )(band, own, lat, weights, b1)


def per_device(
    residual_in,
    cached,
    use_cached,
    queries,
    attn_keys,
    values,
    gate_mod,
    shift_mod,
    scale_mod,
    out_weight,
    final_weight,
    final_bias,
    first_weight,
    first_bias,
    second_weight,
):
    model_width = residual_in.shape[-1]
    channels = first_weight.shape[-1]
    h = lax.axis_index("h").astype(jnp.int32).reshape(1)
    c = lax.axis_index("c").astype(jnp.int32).reshape(1)
    tokens = (x.reshape(TOK, HEADS * HD) for x in (queries, attn_keys, values))
    packed, mine = pack(c, *tokens, out_weight)
    mine = lax.all_gather(mine, "z", axis=0, tiled=True)
    moved = lax.all_to_all(packed, GRP, split_axis=0, concat_axis=0, tiled=True)
    moved = moved.reshape(FRAMES * TOK, 3 * HD)
    kv = jnp.broadcast_to(moved[None, :, HD:], (4, FRAMES * TOK, 2 * HD))
    kv = lax.all_to_all(kv, "ya", split_axis=0, concat_axis=0, tiled=True)
    kv = kv.reshape(4 * FRAMES * TOK, 2 * HD)
    kvs = [kv, lax.ppermute(kv, "c", [(0, 1), (1, 0)])]
    q = jnp.broadcast_to(moved[None, :, :HD], (4, FRAMES * TOK, HD))
    q = lax.all_to_all(q, ("yb", "l"), split_axis=0, concat_axis=0, tiled=True)
    parts = attend(q, kvs)
    parts, mine = lax.optimization_barrier((parts, mine))
    theirs = lax.ppermute(mine, "c", [(0, 1), (1, 0)])
    mine = hold(mine)
    parts = lax.all_to_all(
        parts.reshape(32, 64, HD), ("z", "yb", "l"), split_axis=0, concat_axis=0, tiled=True
    )
    keep, send = project(h, c, parts.reshape(8, 4, 64, HD), mine, theirs)
    recv = lax.all_gather(send, "h", axis=0)
    stream, windows = norm(
        h,
        keep,
        recv,
        residual_in.reshape(TOK, model_width),
        cached.reshape(2, TOK, model_width),
        use_cached.reshape(2, TOK),
        gate_mod[None, :],
        shift_mod[None, :],
        scale_mod[None, :],
        final_weight.T,
        final_bias[None, :],
    )
    windows, w1, w2 = lax.optimization_barrier((windows, first_weight, second_weight))
    lat = lax.all_to_all(
        windows.reshape(512, 2, HD), GRP + COL, split_axis=0, concat_axis=0, tiled=True
    )
    band = lax.axis_index(GRP).astype(jnp.int32).reshape(1)
    own = lax.axis_index(COL).astype(jnp.int32).reshape(1)
    w2 = jnp.transpose(w2, (1, 2, 3, 0, 4)).reshape(27 * 16, channels)
    weights = ready(w1.reshape(27 * 16, channels), w2)
    out = conv(band, own, lat, weights, first_bias[None, :])
    return stream.reshape(residual_in.shape), jnp.transpose(out, (1, 0, 2))


def solution(mesh):
    fine = Mesh(mesh.devices.reshape(2, 8, 4, 2, 2, 2), GRP + COL)
    return jax.shard_map(
        per_device,
        mesh=fine,
        in_specs=(
            P(GRP, COL, None, None),
            P(None, GRP, COL, None, None),
            P(None, GRP, COL, None),
            P(GRP, COL, None, None),
            P(GRP, COL, None, None),
            P(GRP, COL, None, None),
            P(),
            P(),
            P(),
            P(GRP, None),
            P(),
            P(),
            P(),
            P(),
            P(COL, None, None, None, None),
        ),
        out_specs=(P(GRP, COL, None, None), P(COL, GRP, None)),
        check_vma=False,
    )
```

```python
import math

import jax
import jax.numpy as jnp
from jax import lax
from jax.experimental import pallas as pl
from jax.experimental.pallas import tpu as pltpu
from jax.sharding import Mesh, PartitionSpec as P

HD = 128
HEADS = 16
F32 = jnp.float32
BF16 = jnp.bfloat16
MIB = 1 << 20

TOK = 24
FRAMES = 16
PIX = 1024
KEYS = 768

VMEM = pl.BlockSpec(memory_space=pltpu.VMEM)
SMEM = pl.BlockSpec(memory_space=pltpu.SMEM)

GRP = ("h", "z")
COL = ("ya", "yb", "l", "c")


def dot(a, b, contract):
    return lax.dot_general(a, b, ((contract[0], contract[1]), ((), ())), preferred_element_type=F32)


def pack_kernel(c_ref, q_ref, k_ref, v_ref, weight_ref, out_ref, half_ref):
    half = half_ref.shape[1]
    half_ref[...] = weight_ref[:, pl.ds(pl.multiple_of(c_ref[0] * half, 128), half)]
    for g in range(HEADS):
        cols = slice(g * HD, (g + 1) * HD)
        out_ref[g, :, 0:HD] = q_ref[:, cols]
        out_ref[g, :, HD : 2 * HD] = k_ref[:, cols]
        out_ref[g, :, 2 * HD : 3 * HD] = v_ref[:, cols]


def pack(c, q, k, v, weight):
    return pl.pallas_call(
        pack_kernel,
        out_shape=(
            jax.ShapeDtypeStruct((HEADS, TOK, 3 * HD), BF16),
            jax.ShapeDtypeStruct((weight.shape[0], weight.shape[1] // 2), BF16),
        ),
        in_specs=[SMEM] + [VMEM] * 4,
        out_specs=(VMEM, VMEM),
    )(c, q, k, v, weight)


def attend_kernel(q_ref, kv0_ref, kv1_ref, out_ref):
    scale = math.log2(math.e) / math.sqrt(HD)
    half = kv0_ref.shape[0]
    token = lax.broadcasted_iota(jnp.int32, (2 * TOK, HD), 0)
    lane = lax.broadcasted_iota(jnp.int32, (2 * TOK, HD), 1)
    base = lane - lax.rem(token, 6) * 3
    row = lax.broadcasted_iota(jnp.int32, (8, 2 * TOK), 0)
    spot = lax.broadcasted_iota(jnp.int32, (8, 2 * TOK), 1)
    pick = jnp.where(lax.div(spot, 6) == row, 1.0, 0.0).astype(BF16)
    runs = [(ref, slice(at, at + KEYS)) for ref in (kv0_ref, kv1_ref) for at in range(0, half, KEYS)]

    def column(i, carry):
        q = q_ref[i]

        def scores(n):
            ref, rows = runs[n]
            return dot(q, ref[rows, 0:HD], ((1,), (1,)))

        ahead = scores(0)
        top = total = o = None
        for n, (ref, rows) in enumerate(runs):
            s = ahead
            if n + 1 < len(runs):
                ahead = scores(n + 1)
            high = jnp.max(s, axis=1, keepdims=True) * scale
            if n:
                before = top
                top = jnp.maximum(before, high)
                shrink = jnp.exp2(before - top)
            else:
                top = high
            p = jnp.exp2(s * scale - top)
            here = jnp.sum(p, axis=1, keepdims=True)
            part = dot(p.astype(BF16), ref[rows, HD : 2 * HD], ((1,), (0,)))
            total = total * shrink + here if n else here
            o = o * shrink + part if n else part
        o = (o / total).reshape(2, 8, TOK, HD)
        log = top + jnp.log2(total)
        hi = log.astype(BF16).astype(F32)
        mid = (log - hi).astype(BF16).astype(F32)
        lo = log - hi - mid
        hi, mid, lo = (x.reshape(2, 8, TOK, 1) for x in (hi, mid, lo))
        for z in range(8):
            piece = [jnp.concatenate([x[0, z], x[1, z]], axis=0) for x in (hi, mid, lo)]
            spread = jnp.where(
                base == 0,
                piece[0],
                jnp.where(base == 1, piece[1], jnp.where(base == 2, piece[2], 0.0)),
            )
            stats = dot(pick, spread.astype(BF16), ((1,), (0,)))
            out_ref[z, i] = jnp.concatenate([o[0, z], o[1, z], stats], axis=0).astype(BF16)
        return carry

    lax.fori_loop(0, 4, column, 0)


def attend(q, kvs):
    return pl.pallas_call(
        attend_kernel,
        out_shape=jax.ShapeDtypeStruct((8, 4, 56, HD), BF16),
        in_specs=[VMEM] * 3,
        out_specs=VMEM,
        compiler_params=pltpu.CompilerParams(vmem_limit_bytes=32 * MIB),
    )(q, *kvs)


def hold_kernel(own_ref, out_ref, sem):
    copy = pltpu.make_async_copy(own_ref, out_ref, sem)
    copy.start()
    copy.wait()


def hold(own):
    return pl.pallas_call(
        hold_kernel,
        out_shape=jax.ShapeDtypeStruct(own.shape, BF16),
        in_specs=[pl.BlockSpec(memory_space=pltpu.HBM)],
        out_specs=VMEM,
        scratch_shapes=[pltpu.SemaphoreType.DMA],
        cost_estimate=pl.CostEstimate(flops=0, bytes_accessed=2 * own.size * 2, transcendentals=0),
        compiler_params=pltpu.CompilerParams(vmem_limit_bytes=8 * MIB),
    )(own)


def project_kernel(h_ref, c_ref, parts_ref, own_ref, other_ref, keep_ref, send_ref, att_ref, sum_ref):
    step = pl.program_id(0)

    @pl.when(step == 0)
    def join():
        join_parts(parts_ref, att_ref)

    @pl.when(step < 2)
    def near():
        sum_ref[...] = dot(att_ref[...], own_ref[...], ((1,), (0,)))

    @pl.when(step >= 2)
    def far():
        sum_ref[...] = dot(att_ref[...], other_ref[...], ((1,), (0,)))

    h = h_ref[0]
    keep_ref[...] = sum_ref[pl.ds(pl.multiple_of(h * TOK, 8), TOK), :]
    send_ref[...] = sum_ref[pl.ds(pl.multiple_of((1 - h) * TOK, 8), TOK), :].astype(BF16)


def join_parts(parts_ref, att_ref):
    token = lax.broadcasted_iota(jnp.int32, (2 * TOK, HD), 0)
    lane = lax.broadcasted_iota(jnp.int32, (2 * TOK, HD), 1)
    base = lane - lax.rem(token, 6) * 3
    mine = (base >= 0) & (base < 3)
    spot = lax.broadcasted_iota(jnp.int32, (2 * TOK, 8), 0)
    row = lax.broadcasted_iota(jnp.int32, (2 * TOK, 8), 1)
    pick = jnp.where(lax.div(spot, 6) == row, 1.0, 0.0).astype(BF16)
    for z in range(8):
        logs = []
        pieces = [parts_ref[z, j].astype(F32) for j in range(4)]
        for j in range(4):
            spread = dot(pick, pieces[j][48:56].astype(BF16), ((1,), (0,)))
            logs.append(jnp.sum(jnp.where(mine, spread, 0.0), axis=1, keepdims=True))
        top = jnp.maximum(jnp.maximum(logs[0], logs[1]), jnp.maximum(logs[2], logs[3]))
        shares = [jnp.exp2(x - top) for x in logs]
        total = (shares[0] + shares[1]) + (shares[2] + shares[3])
        att = jnp.zeros((2 * TOK, HD), F32)
        for j in range(4):
            att = att + pieces[j][0:48] * (shares[j] / total)
        att_ref[:, z * HD : (z + 1) * HD] = att.astype(BF16)


def project(h, c, parts, own, other):
    depth, half = own.shape
    block = half // 2

    def place(i, h_ref, c_ref):
        side = jnp.where(i < 2, c_ref[0], 1 - c_ref[0])
        return 0, side * 2 + lax.rem(i, 2)

    return pl.pallas_call(
        project_kernel,
        out_shape=(
            jax.ShapeDtypeStruct((TOK, 2 * half), F32),
            jax.ShapeDtypeStruct((TOK, 2 * half), BF16),
        ),
        grid_spec=pltpu.PrefetchScalarGridSpec(
            num_scalar_prefetch=2,
            grid=(4,),
            in_specs=[
                pl.BlockSpec(parts.shape, lambda i, h_ref, c_ref: (0, 0, 0, 0)),
                pl.BlockSpec((depth, block), lambda i, h_ref, c_ref: (0, jnp.minimum(i, 1))),
                pl.BlockSpec((depth, block), lambda i, h_ref, c_ref: (0, jnp.maximum(i - 2, 0))),
            ],
            out_specs=(pl.BlockSpec((TOK, block), place), pl.BlockSpec((TOK, block), place)),
            scratch_shapes=[
                pltpu.VMEM((2 * TOK, depth), BF16),
                pltpu.VMEM((2 * TOK, block), F32),
            ],
        ),
        compiler_params=pltpu.CompilerParams(vmem_limit_bytes=24 * MIB),
    )(h, c, parts, own, other)


def norm_kernel(
    h_ref, keep_ref, recv_ref, res_ref, cached_ref, use_ref, gate_ref, shift_ref, scale_ref, fw_ref, fb_ref,
    stream_ref, out_ref,
):
    eye = lax.broadcasted_iota(jnp.int32, (TOK, TOK), 0) == lax.broadcasted_iota(
        jnp.int32, (TOK, TOK), 1
    )
    mixed = res_ref[...].astype(F32)
    for b in range(2):
        used = use_ref[b : b + 1, :].astype(F32)
        column = jnp.sum(jnp.where(eye, used, 0.0), axis=1, keepdims=True)
        mixed = mixed + column * cached_ref[b].astype(F32)
    projected = keep_ref[...] + recv_ref[1 - h_ref[0]].astype(F32)
    stream = (mixed + gate_ref[...] * projected).astype(BF16)
    stream_ref[...] = stream
    x = stream.astype(F32)
    center = jnp.mean(x, axis=1, keepdims=True)
    off = x - center
    spread = jnp.mean(off * off, axis=1, keepdims=True)
    modulated = off * lax.rsqrt(spread + 1e-6) * (1.0 + scale_ref[...]) + shift_ref[...]
    latent = dot(modulated.astype(BF16), fw_ref[...], ((1,), (1,))) + fb_ref[...]
    latent = latent.astype(BF16)
    source = lax.broadcasted_iota(jnp.int32, (64, 64), 0)
    target = lax.broadcasted_iota(jnp.int32, (64, 64), 1)
    group = lax.div(target, 16)
    wanted = (lax.rem(group, 2) * 2 + lax.div(group, 2)) * 16 + lax.rem(target, 16)
    latent = dot(latent, jnp.where(source == wanted, 1.0, 0.0).astype(BF16), ((1,), (0,)))
    latent = latent.astype(BF16)
    band = lax.broadcasted_iota(jnp.int32, (FRAMES, TOK), 0)
    source = lax.broadcasted_iota(jnp.int32, (FRAMES, TOK), 1)
    first = lax.div(3 * band, 2) - 1
    pieces = [
        dot(jnp.where(source == first + k, 1.0, 0.0).astype(BF16), latent, ((1,), (0,)))
        for k in range(4)
    ]
    window = [x[:, 0:32] for x in pieces] + [x[:, 32:64] for x in pieces]
    window = jnp.concatenate(window, axis=1).reshape(FRAMES, 1, 2, HD)
    out_ref[...] = jnp.broadcast_to(window, (FRAMES, 32, 2, HD)).astype(BF16)


def norm(h, keep, recv, res, cached, use, gate, shift, scale, fw, fb):
    return pl.pallas_call(
        norm_kernel,
        out_shape=(
            jax.ShapeDtypeStruct(res.shape, BF16),
            jax.ShapeDtypeStruct((FRAMES, 32, 2, HD), BF16),
        ),
        in_specs=[SMEM] + [VMEM] * 10,
        out_specs=(VMEM, VMEM),
        compiler_params=pltpu.CompilerParams(vmem_limit_bytes=32 * MIB),
    )(h, keep, recv, res, cached, use, gate, shift, scale, fw, fb)


def frames_back(x, count, lane):
    if count == 0:
        return x
    moved = pltpu.roll(x, 64 * count, 1)
    start = x[:, 0:128]
    start = jnp.where(lane[:, 0:128] < 64, start, pltpu.roll(start, 64, 1))
    width = 128
    head = jnp.where(lane[:, 0:width] < 64 * count, start, moved[:, 0:width])
    return jnp.concatenate([head, moved[:, width:]], axis=1)


def column_shift(x, by, place):
    if by == 0:
        return x
    moved = pltpu.roll(x, (-by) % PIX, 1)
    edge = 63 if by == 1 else 0
    return jnp.where(place == edge, 0.0, moved)


def ready_kernel(w1_ref, w2_ref, out_ref):
    taps = w2_ref.shape[0]
    out_ref[0:taps, :] = w2_ref[...]
    out_ref[taps:, 0:taps] = jnp.transpose(w1_ref[...].astype(F32)).astype(BF16)


def ready(w1, w2):
    return pl.pallas_call(
        ready_kernel,
        out_shape=jax.ShapeDtypeStruct((432 + 512, 512), BF16),
        in_specs=[VMEM] * 2,
        out_specs=VMEM,
        cost_estimate=pl.CostEstimate(flops=0, bytes_accessed=1 << 23, transcendentals=0),
        compiler_params=pltpu.CompilerParams(vmem_limit_bytes=8 * MIB),
    )(w1, w2)


def conv_kernel(band_ref, own_ref, lat_ref, weights_ref, b1_ref, out_ref, taps_ref, first_ref, acc_ref):
    band = band_ref[0]
    lanes = own_ref[0]
    bias = jnp.transpose(jnp.broadcast_to(b1_ref[...], (8, 512)))[:, 0:1]
    lane16 = lax.broadcasted_iota(jnp.int32, (16, PIX), 1)
    place16 = lax.rem(lane16, 64)
    latent = jnp.transpose(lat_ref[...].astype(F32).reshape(PIX, 128))
    latent = jnp.where(lax.rem(band, 2) == 1, latent[16:128], latent[0:112])
    for r in range(7):
        row = latent[r * 16 : r * 16 + 16]
        for b in range(3):
            moved = column_shift(row, b - 1, place16)
            for t in range(3):
                at = r * 48 + b * 16
                taps_ref[t, at : at + 16, :] = frames_back(moved, 2 - t, lane16).astype(BF16)
    acc_ref[...] = jnp.zeros_like(acc_ref)
    for r in range(5):
        patches = jnp.concatenate([taps_ref[t, r * 48 : r * 48 + 144, :] for t in range(3)], axis=0)
        first = dot(weights_ref[432:, 0:432], patches, ((1,), (0,))) + bias
        height = 3 * band - 1 + r
        inside = jnp.where((height >= 0) & (height < 48), 1.0, 0.0)
        rounded = (first * inside).astype(BF16)
        v = rounded.astype(F32)
        if 1 <= r <= 3:
            first_ref[r - 1] = rounded
        half = 0.5 * v
        act = (half * jnp.tanh(half) + half).astype(BF16)
        low, high = max(r - 2, 0), min(r, 2)
        z = dot(weights_ref[low * 144 : (high + 1) * 144, :], act, ((1,), (0,)))
        for a in range(low, high + 1):
            for t in range(3):
                at = ((a - low) * 3 + t) * 48
                acc_ref[r - a, t] += z[at : at + 48]
    for o in range(3):
        own = pl.ds(pl.multiple_of(lanes * 16, 16), 16)
        total = first_ref[o, own, :].astype(F32)
        for t in range(3):
            u = acc_ref[o, t, 16:32, :]
            u = u + column_shift(acc_ref[o, t, 0:16, :], -1, place16)
            u = u + column_shift(acc_ref[o, t, 32:48, :], 1, place16)
            u = frames_back(u, 2 - t, lane16)
            total = total + u
        out_ref[o] = total.astype(BF16)


def conv(band, own, lat, weights, b1):
    return pl.pallas_call(
        conv_kernel,
        out_shape=jax.ShapeDtypeStruct((3, 16, PIX), BF16),
        in_specs=[SMEM] * 2 + [VMEM] * 3,
        out_specs=VMEM,
        scratch_shapes=[
            pltpu.VMEM((3, 7 * 48, PIX), BF16),
            pltpu.VMEM((3, 512, PIX), BF16),
            pltpu.VMEM((3, 3, 48, PIX), F32),
        ],
        compiler_params=pltpu.CompilerParams(vmem_limit_bytes=28 * MIB),
    )(band, own, lat, weights, b1)


def per_device(
    residual_in,
    cached,
    use_cached,
    queries,
    attn_keys,
    values,
    gate_mod,
    shift_mod,
    scale_mod,
    out_weight,
    final_weight,
    final_bias,
    first_weight,
    first_bias,
    second_weight,
):
    model_width = residual_in.shape[-1]
    channels = first_weight.shape[-1]
    h = lax.axis_index("h").astype(jnp.int32).reshape(1)
    c = lax.axis_index("c").astype(jnp.int32).reshape(1)
    tokens = (x.reshape(TOK, HEADS * HD) for x in (queries, attn_keys, values))
    packed, mine = pack(c, *tokens, out_weight)
    mine = lax.all_gather(mine, "z", axis=0, tiled=True)
    moved = lax.all_to_all(packed, GRP, split_axis=0, concat_axis=0, tiled=True)
    moved = moved.reshape(FRAMES * TOK, 3 * HD)
    kv = jnp.broadcast_to(moved[None, :, HD:], (4, FRAMES * TOK, 2 * HD))
    kv = lax.all_to_all(kv, "ya", split_axis=0, concat_axis=0, tiled=True)
    kv = kv.reshape(4 * FRAMES * TOK, 2 * HD)
    kvs = [kv, lax.ppermute(kv, "c", [(0, 1), (1, 0)])]
    q = jnp.broadcast_to(moved[None, :, :HD], (4, FRAMES * TOK, HD))
    q = lax.all_to_all(q, ("yb", "l"), split_axis=0, concat_axis=0, tiled=True)
    parts = attend(q, kvs)
    parts, mine = lax.optimization_barrier((parts, mine))
    theirs = lax.ppermute(mine, "c", [(0, 1), (1, 0)])
    mine = hold(mine)
    parts = lax.all_to_all(
        parts.reshape(32, 56, HD), ("z", "yb", "l"), split_axis=0, concat_axis=0, tiled=True
    )
    keep, send = project(h, c, parts.reshape(8, 4, 56, HD), mine, theirs)
    recv = lax.all_gather(send, "h", axis=0)
    stream, windows = norm(
        h,
        keep,
        recv,
        residual_in.reshape(TOK, model_width),
        cached.reshape(2, TOK, model_width),
        use_cached.reshape(2, TOK),
        gate_mod[None, :],
        shift_mod[None, :],
        scale_mod[None, :],
        final_weight.T,
        final_bias[None, :],
    )
    windows, w1, w2 = lax.optimization_barrier((windows, first_weight, second_weight))
    lat = lax.all_to_all(
        windows.reshape(512, 2, HD), GRP + COL, split_axis=0, concat_axis=0, tiled=True
    )
    band = lax.axis_index(GRP).astype(jnp.int32).reshape(1)
    own = lax.axis_index(COL).astype(jnp.int32).reshape(1)
    w2 = jnp.transpose(w2, (2, 1, 3, 0, 4)).reshape(27 * 16, channels)
    weights = ready(w1.reshape(27 * 16, channels), w2)
    out = conv(band, own, lat, weights, first_bias[None, :])
    return stream.reshape(residual_in.shape), jnp.transpose(out, (1, 0, 2))


def solution(mesh):
    fine = Mesh(mesh.devices.reshape(2, 8, 4, 2, 2, 2), GRP + COL)
    return jax.shard_map(
        per_device,
        mesh=fine,
        in_specs=(
            P(GRP, COL, None, None),
            P(None, GRP, COL, None, None),
            P(None, GRP, COL, None),
            P(GRP, COL, None, None),
            P(GRP, COL, None, None),
            P(GRP, COL, None, None),
            P(),
            P(),
            P(),
            P(GRP, None),
            P(),
            P(),
            P(),
            P(),
            P(COL, None, None, None, None),
        ),
        out_specs=(P(GRP, COL, None, None), P(COL, GRP, None)),
        check_vma=False,
    )
```

```python
import math

import jax
import jax.numpy as jnp
from jax import lax
from jax.experimental import pallas as pl
from jax.experimental.pallas import tpu as pltpu
from jax.sharding import Mesh, PartitionSpec as P

HD = 128
HEADS = 16
F32 = jnp.float32
BF16 = jnp.bfloat16
MIB = 1 << 20

TOK = 24
FRAMES = 16
PIX = 1024
KEYS = 768

VMEM = pl.BlockSpec(memory_space=pltpu.VMEM)
SMEM = pl.BlockSpec(memory_space=pltpu.SMEM)

GRP = ("h", "z")
COL = ("ya", "yb", "l", "c")


def dot(a, b, contract):
    return lax.dot_general(a, b, ((contract[0], contract[1]), ((), ())), preferred_element_type=F32)


def pack_kernel(c_ref, q_ref, k_ref, v_ref, weight_ref, out_ref, half_ref):
    half_ref[...] = weight_ref[...]
    for g in range(out_ref.shape[0]):
        cols = slice(g * HD, (g + 1) * HD)
        out_ref[g, :, 0:HD] = q_ref[:, cols]
        out_ref[g, :, HD : 2 * HD] = k_ref[:, cols]
        out_ref[g, :, 2 * HD : 3 * HD] = v_ref[:, cols]


def pack(c, q, k, v, weight):
    depth, width = weight.shape
    steps = 2
    tokens = pl.BlockSpec((TOK, HEADS * HD // steps), lambda i, c_ref: (0, i))
    return pl.pallas_call(
        pack_kernel,
        out_shape=(
            jax.ShapeDtypeStruct((HEADS, TOK, 3 * HD), BF16),
            jax.ShapeDtypeStruct((depth, width // 2), BF16),
        ),
        grid_spec=pltpu.PrefetchScalarGridSpec(
            num_scalar_prefetch=1,
            grid=(steps,),
            in_specs=[tokens] * 3
            + [pl.BlockSpec((depth // steps, width // 2), lambda i, c_ref: (i, c_ref[0]))],
            out_specs=(
                pl.BlockSpec((HEADS // steps, TOK, 3 * HD), lambda i, c_ref: (i, 0, 0)),
                pl.BlockSpec((depth // steps, width // 2), lambda i, c_ref: (i, 0)),
            ),
        ),
    )(c, q, k, v, weight)


def attend_kernel(q_ref, kv0_ref, kv1_ref, out_ref):
    scale = math.log2(math.e) / math.sqrt(HD)
    half = kv0_ref.shape[0]
    token = lax.broadcasted_iota(jnp.int32, (2 * TOK, HD), 0)
    lane = lax.broadcasted_iota(jnp.int32, (2 * TOK, HD), 1)
    base = lane - lax.rem(token, 6) * 3
    row = lax.broadcasted_iota(jnp.int32, (8, 2 * TOK), 0)
    spot = lax.broadcasted_iota(jnp.int32, (8, 2 * TOK), 1)
    pick = jnp.where(lax.div(spot, 6) == row, 1.0, 0.0).astype(BF16)
    runs = [(ref, slice(at, at + KEYS)) for ref in (kv0_ref, kv1_ref) for at in range(0, half, KEYS)]

    def column(i, carry):
        q = q_ref[i]

        def scores(n):
            ref, rows = runs[n]
            return dot(q, ref[rows, 0:HD], ((1,), (1,)))

        ahead = scores(0)
        top = total = o = None
        for n, (ref, rows) in enumerate(runs):
            s = ahead
            if n + 1 < len(runs):
                ahead = scores(n + 1)
            high = jnp.max(s, axis=1, keepdims=True) * scale
            if n:
                before = top
                top = jnp.maximum(before, high)
                shrink = jnp.exp2(before - top)
            else:
                top = high
            p = jnp.exp2(s * scale - top)
            here = jnp.sum(p, axis=1, keepdims=True)
            part = dot(p.astype(BF16), ref[rows, HD : 2 * HD], ((1,), (0,)))
            total = total * shrink + here if n else here
            o = o * shrink + part if n else part
        o = (o / total).reshape(2, 8, TOK, HD)
        log = top + jnp.log2(total)
        hi = log.astype(BF16).astype(F32)
        mid = (log - hi).astype(BF16).astype(F32)
        lo = log - hi - mid
        hi, mid, lo = (x.reshape(2, 8, TOK, 1) for x in (hi, mid, lo))
        for z in range(8):
            piece = [jnp.concatenate([x[0, z], x[1, z]], axis=0) for x in (hi, mid, lo)]
            spread = jnp.where(
                base == 0,
                piece[0],
                jnp.where(base == 1, piece[1], jnp.where(base == 2, piece[2], 0.0)),
            )
            stats = dot(pick, spread.astype(BF16), ((1,), (0,)))
            out_ref[z, i] = jnp.concatenate([o[0, z], o[1, z], stats], axis=0).astype(BF16)
        return carry

    lax.fori_loop(0, 4, column, 0)


def attend(q, kvs):
    return pl.pallas_call(
        attend_kernel,
        out_shape=jax.ShapeDtypeStruct((8, 4, 56, HD), BF16),
        in_specs=[VMEM] * 3,
        out_specs=VMEM,
        compiler_params=pltpu.CompilerParams(vmem_limit_bytes=32 * MIB),
    )(q, *kvs)


def project_kernel(
    h_ref, c_ref, parts_ref, own_ref, other_ref, keep_ref, send_ref,
    near_ref, far_ref, att_ref, sum_ref, part_sems, far_sems,
):
    step = pl.program_id(0)
    block = sum_ref.shape[1]

    def far_copy(n):
        return pltpu.make_async_copy(
            other_ref.at[:, n * block : (n + 1) * block], far_ref.at[n], far_sems.at[n]
        )

    @pl.when(step == 0)
    def join():
        copies = [
            pltpu.make_async_copy(
                parts_ref.at[pl.ds(n * 4, 4)], near_ref.at[pl.ds(n * 4, 4)], part_sems.at[n]
            )
            for n in range(2)
        ]
        for copy in copies:
            copy.start()
        for n in range(2):
            far_copy(n).start()
        for n, copy in enumerate(copies):
            copy.wait()
            join_parts(near_ref, att_ref, range(n * 4, n * 4 + 4))

    @pl.when(step < 2)
    def near():
        sum_ref[...] = dot(att_ref[...], own_ref[...], ((1,), (0,)))

    for n in range(2):

        @pl.when(step == 2 + n)
        def far(n=n):
            far_copy(n).wait()
            sum_ref[...] = dot(att_ref[...], far_ref[n], ((1,), (0,)))

    h = h_ref[0]
    keep_ref[...] = sum_ref[pl.ds(pl.multiple_of(h * TOK, 8), TOK), :]
    send_ref[...] = sum_ref[pl.ds(pl.multiple_of((1 - h) * TOK, 8), TOK), :].astype(BF16)


def join_parts(parts_ref, att_ref, heads):
    token = lax.broadcasted_iota(jnp.int32, (2 * TOK, HD), 0)
    lane = lax.broadcasted_iota(jnp.int32, (2 * TOK, HD), 1)
    base = lane - lax.rem(token, 6) * 3
    mine = (base >= 0) & (base < 3)
    spot = lax.broadcasted_iota(jnp.int32, (2 * TOK, 8), 0)
    row = lax.broadcasted_iota(jnp.int32, (2 * TOK, 8), 1)
    pick = jnp.where(lax.div(spot, 6) == row, 1.0, 0.0).astype(BF16)
    for z in heads:
        logs = []
        pieces = [parts_ref[z, j].astype(F32) for j in range(4)]
        for j in range(4):
            spread = dot(pick, pieces[j][48:56].astype(BF16), ((1,), (0,)))
            logs.append(jnp.sum(jnp.where(mine, spread, 0.0), axis=1, keepdims=True))
        top = jnp.maximum(jnp.maximum(logs[0], logs[1]), jnp.maximum(logs[2], logs[3]))
        shares = [jnp.exp2(x - top) for x in logs]
        total = (shares[0] + shares[1]) + (shares[2] + shares[3])
        att = jnp.zeros((2 * TOK, HD), F32)
        for j in range(4):
            att = att + pieces[j][0:48] * (shares[j] / total)
        att_ref[:, z * HD : (z + 1) * HD] = att.astype(BF16)


def project(h, c, parts, own, other):
    depth, half = own.shape
    block = half // 2

    def place(i, h_ref, c_ref):
        side = jnp.where(i < 2, c_ref[0], 1 - c_ref[0])
        return 0, side * 2 + lax.rem(i, 2)

    return pl.pallas_call(
        project_kernel,
        out_shape=(
            jax.ShapeDtypeStruct((TOK, 2 * half), F32),
            jax.ShapeDtypeStruct((TOK, 2 * half), BF16),
        ),
        grid_spec=pltpu.PrefetchScalarGridSpec(
            num_scalar_prefetch=2,
            grid=(4,),
            in_specs=[
                pl.BlockSpec(memory_space=pl.ANY),
                pl.BlockSpec((depth, block), lambda i, h_ref, c_ref: (0, jnp.minimum(i, 1))),
                pl.BlockSpec(memory_space=pl.ANY),
            ],
            out_specs=(pl.BlockSpec((TOK, block), place), pl.BlockSpec((TOK, block), place)),
            scratch_shapes=[
                pltpu.VMEM(parts.shape, BF16),
                pltpu.VMEM((2, depth, block), BF16),
                pltpu.VMEM((2 * TOK, depth), BF16),
                pltpu.VMEM((2 * TOK, block), F32),
                pltpu.SemaphoreType.DMA((2,)),
                pltpu.SemaphoreType.DMA((2,)),
            ],
        ),
        compiler_params=pltpu.CompilerParams(vmem_limit_bytes=24 * MIB),
    )(h, c, parts, own, other)


def norm_kernel(
    h_ref, keep_ref, recv_ref, res_ref, cached_ref, use_ref, gate_ref, shift_ref, scale_ref, fw_ref, fb_ref,
    stream_ref, out_ref,
):
    eye = lax.broadcasted_iota(jnp.int32, (TOK, TOK), 0) == lax.broadcasted_iota(
        jnp.int32, (TOK, TOK), 1
    )
    mixed = res_ref[...].astype(F32)
    for b in range(2):
        used = use_ref[b : b + 1, :].astype(F32)
        column = jnp.sum(jnp.where(eye, used, 0.0), axis=1, keepdims=True)
        mixed = mixed + column * cached_ref[b].astype(F32)
    projected = keep_ref[...] + recv_ref[1 - h_ref[0]].astype(F32)
    stream = (mixed + gate_ref[...] * projected).astype(BF16)
    stream_ref[...] = stream
    x = stream.astype(F32)
    center = jnp.mean(x, axis=1, keepdims=True)
    off = x - center
    spread = jnp.mean(off * off, axis=1, keepdims=True)
    modulated = off * lax.rsqrt(spread + 1e-6) * (1.0 + scale_ref[...]) + shift_ref[...]
    latent = dot(modulated.astype(BF16), fw_ref[...], ((1,), (1,))) + fb_ref[...]
    latent = latent.astype(BF16)
    source = lax.broadcasted_iota(jnp.int32, (64, 64), 0)
    target = lax.broadcasted_iota(jnp.int32, (64, 64), 1)
    group = lax.div(target, 16)
    wanted = (lax.rem(group, 2) * 2 + lax.div(group, 2)) * 16 + lax.rem(target, 16)
    latent = dot(latent, jnp.where(source == wanted, 1.0, 0.0).astype(BF16), ((1,), (0,)))
    latent = latent.astype(BF16)
    band = lax.broadcasted_iota(jnp.int32, (FRAMES, TOK), 0)
    source = lax.broadcasted_iota(jnp.int32, (FRAMES, TOK), 1)
    first = lax.div(3 * band, 2) - 1
    pieces = [
        dot(jnp.where(source == first + k, 1.0, 0.0).astype(BF16), latent, ((1,), (0,)))
        for k in range(4)
    ]
    window = [x[:, 0:32] for x in pieces] + [x[:, 32:64] for x in pieces]
    window = jnp.concatenate(window, axis=1).reshape(FRAMES, 1, 2, HD)
    out_ref[...] = jnp.broadcast_to(window, (FRAMES, 32, 2, HD)).astype(BF16)


def norm(h, keep, recv, res, cached, use, gate, shift, scale, fw, fb):
    return pl.pallas_call(
        norm_kernel,
        out_shape=(
            jax.ShapeDtypeStruct(res.shape, BF16),
            jax.ShapeDtypeStruct((FRAMES, 32, 2, HD), BF16),
        ),
        in_specs=[SMEM] + [VMEM] * 10,
        out_specs=(VMEM, VMEM),
        compiler_params=pltpu.CompilerParams(vmem_limit_bytes=32 * MIB),
    )(h, keep, recv, res, cached, use, gate, shift, scale, fw, fb)


def frames_back(x, count, lane):
    if count == 0:
        return x
    moved = pltpu.roll(x, 64 * count, 1)
    start = x[:, 0:128]
    start = jnp.where(lane[:, 0:128] < 64, start, pltpu.roll(start, 64, 1))
    width = 128
    head = jnp.where(lane[:, 0:width] < 64 * count, start, moved[:, 0:width])
    return jnp.concatenate([head, moved[:, width:]], axis=1)


def column_shift(x, by, place):
    if by == 0:
        return x
    moved = pltpu.roll(x, (-by) % PIX, 1)
    edge = 63 if by == 1 else 0
    return jnp.where(place == edge, 0.0, moved)


def ready_kernel(w1_ref, w2_ref, out_ref):
    taps = w2_ref.shape[0]
    out_ref[0:taps, :] = w2_ref[...]
    out_ref[taps:, 0:taps] = jnp.transpose(w1_ref[...].astype(F32)).astype(BF16)


def ready(w1, w2):
    return pl.pallas_call(
        ready_kernel,
        out_shape=jax.ShapeDtypeStruct((432 + 512, 512), BF16),
        in_specs=[VMEM] * 2,
        out_specs=VMEM,
        cost_estimate=pl.CostEstimate(flops=0, bytes_accessed=1 << 23, transcendentals=0),
        compiler_params=pltpu.CompilerParams(vmem_limit_bytes=8 * MIB),
    )(w1, w2)


def conv_kernel(band_ref, own_ref, lat_ref, weights_ref, b1_ref, out_ref, taps_ref, first_ref, acc_ref):
    band = band_ref[0]
    lanes = own_ref[0]
    bias = jnp.transpose(jnp.broadcast_to(b1_ref[...], (8, 512)))[:, 0:1]
    lane16 = lax.broadcasted_iota(jnp.int32, (16, PIX), 1)
    place16 = lax.rem(lane16, 64)
    latent = jnp.transpose(lat_ref[...].astype(F32).reshape(PIX, 128))
    latent = jnp.where(lax.rem(band, 2) == 1, latent[16:128], latent[0:112])
    for r in range(7):
        row = latent[r * 16 : r * 16 + 16]
        for b in range(3):
            moved = column_shift(row, b - 1, place16)
            for t in range(3):
                at = r * 48 + b * 16
                taps_ref[t, at : at + 16, :] = frames_back(moved, 2 - t, lane16).astype(BF16)
    acc_ref[...] = jnp.zeros_like(acc_ref)
    for r in range(5):
        patches = jnp.concatenate([taps_ref[t, r * 48 : r * 48 + 144, :] for t in range(3)], axis=0)
        first = dot(weights_ref[432:, 0:432], patches, ((1,), (0,))) + bias
        height = 3 * band - 1 + r
        inside = jnp.where((height >= 0) & (height < 48), 1.0, 0.0)
        rounded = (first * inside).astype(BF16)
        v = rounded.astype(F32)
        if 1 <= r <= 3:
            first_ref[r - 1] = rounded
        half = 0.5 * v
        act = (half * jnp.tanh(half) + half).astype(BF16)
        low, high = max(r - 2, 0), min(r, 2)
        z = dot(weights_ref[low * 144 : (high + 1) * 144, :], act, ((1,), (0,)))
        for a in range(low, high + 1):
            for t in range(3):
                at = ((a - low) * 3 + t) * 48
                acc_ref[r - a, t] += z[at : at + 48]
    for o in range(3):
        own = pl.ds(pl.multiple_of(lanes * 16, 16), 16)
        total = first_ref[o, own, :].astype(F32)
        for t in range(3):
            u = acc_ref[o, t, 16:32, :]
            u = u + column_shift(acc_ref[o, t, 0:16, :], -1, place16)
            u = u + column_shift(acc_ref[o, t, 32:48, :], 1, place16)
            u = frames_back(u, 2 - t, lane16)
            total = total + u
        out_ref[o] = total.astype(BF16)


def conv(band, own, lat, weights, b1):
    return pl.pallas_call(
        conv_kernel,
        out_shape=jax.ShapeDtypeStruct((3, 16, PIX), BF16),
        in_specs=[SMEM] * 2 + [VMEM] * 3,
        out_specs=VMEM,
        scratch_shapes=[
            pltpu.VMEM((3, 7 * 48, PIX), BF16),
            pltpu.VMEM((3, 512, PIX), BF16),
            pltpu.VMEM((3, 3, 48, PIX), F32),
        ],
        compiler_params=pltpu.CompilerParams(vmem_limit_bytes=28 * MIB),
    )(band, own, lat, weights, b1)


def per_device(
    residual_in,
    cached,
    use_cached,
    queries,
    attn_keys,
    values,
    gate_mod,
    shift_mod,
    scale_mod,
    out_weight,
    final_weight,
    final_bias,
    first_weight,
    first_bias,
    second_weight,
):
    model_width = residual_in.shape[-1]
    channels = first_weight.shape[-1]
    h = lax.axis_index("h").astype(jnp.int32).reshape(1)
    c = lax.axis_index("c").astype(jnp.int32).reshape(1)
    tokens = (x.reshape(TOK, HEADS * HD) for x in (queries, attn_keys, values))
    packed, mine = pack(c, *tokens, out_weight)
    mine = lax.all_gather(mine, "z", axis=0, tiled=True)
    moved = lax.all_to_all(packed, GRP, split_axis=0, concat_axis=0, tiled=True)
    moved = moved.reshape(FRAMES * TOK, 3 * HD)
    kv = jnp.broadcast_to(moved[None, :, HD:], (4, FRAMES * TOK, 2 * HD))
    kv = lax.all_to_all(kv, "ya", split_axis=0, concat_axis=0, tiled=True)
    kv = kv.reshape(4 * FRAMES * TOK, 2 * HD)
    kvs = [kv, lax.ppermute(kv, "c", [(0, 1), (1, 0)])]
    q = jnp.broadcast_to(moved[None, :, :HD], (4, FRAMES * TOK, HD))
    q = lax.all_to_all(q, ("yb", "l"), split_axis=0, concat_axis=0, tiled=True)
    parts = attend(q, kvs)
    parts, mine = lax.optimization_barrier((parts, mine))
    theirs = lax.ppermute(mine, "c", [(0, 1), (1, 0)])
    one = jnp.where(c[0] >= 0, 1.0, 0.0).astype(BF16)
    mine = mine * one
    parts = lax.all_to_all(
        parts.reshape(32, 56, HD), ("z", "yb", "l"), split_axis=0, concat_axis=0, tiled=True
    )
    keep, send = project(h, c, parts.reshape(8, 4, 56, HD), mine, theirs)
    recv = lax.all_gather(send, "h", axis=0)
    stream, windows = norm(
        h,
        keep,
        recv,
        residual_in.reshape(TOK, model_width),
        cached.reshape(2, TOK, model_width),
        use_cached.reshape(2, TOK),
        gate_mod[None, :],
        shift_mod[None, :],
        scale_mod[None, :],
        final_weight.T,
        final_bias[None, :],
    )
    windows, w1, w2 = lax.optimization_barrier((windows, first_weight, second_weight))
    lat = lax.all_to_all(
        windows.reshape(512, 2, HD), GRP + COL, split_axis=0, concat_axis=0, tiled=True
    )
    band = lax.axis_index(GRP).astype(jnp.int32).reshape(1)
    own = lax.axis_index(COL).astype(jnp.int32).reshape(1)
    w2 = jnp.transpose(w2, (2, 1, 3, 0, 4)).reshape(27 * 16, channels)
    weights = ready(w1.reshape(27 * 16, channels), w2)
    out = conv(band, own, lat, weights, first_bias[None, :])
    return stream.reshape(residual_in.shape), jnp.transpose(out, (1, 0, 2))


def solution(mesh):
    fine = Mesh(mesh.devices.reshape(2, 8, 4, 2, 2, 2), GRP + COL)
    return jax.shard_map(
        per_device,
        mesh=fine,
        in_specs=(
            P(GRP, COL, None, None),
            P(None, GRP, COL, None, None),
            P(None, GRP, COL, None),
            P(GRP, COL, None, None),
            P(GRP, COL, None, None),
            P(GRP, COL, None, None),
            P(),
            P(),
            P(),
            P(GRP, None),
            P(),
            P(),
            P(),
            P(),
            P(COL, None, None, None, None),
        ),
        out_specs=(P(GRP, COL, None, None), P(COL, GRP, None)),
        check_vma=False,
    )
```

```python
import math

import jax
import jax.numpy as jnp
from jax import lax
from jax.experimental import pallas as pl
from jax.experimental.pallas import tpu as pltpu
from jax.sharding import Mesh, PartitionSpec as P

HD = 128
HEADS = 16
F32 = jnp.float32
BF16 = jnp.bfloat16
MIB = 1 << 20

TOK = 24
FRAMES = 16
PIX = 1024
KEYS = 768

VMEM = pl.BlockSpec(memory_space=pltpu.VMEM)
SMEM = pl.BlockSpec(memory_space=pltpu.SMEM)

GRP = ("h", "z")
COL = ("ya", "yb", "l", "c")


def dot(a, b, contract):
    return lax.dot_general(a, b, ((contract[0], contract[1]), ((), ())), preferred_element_type=F32)


def pack_kernel(c_ref, q_ref, k_ref, v_ref, weight_ref, out_ref, half_ref):
    half_ref[...] = weight_ref[...]
    for g in range(out_ref.shape[0]):
        cols = slice(g * HD, (g + 1) * HD)
        out_ref[g, :, 0:HD] = q_ref[:, cols]
        out_ref[g, :, HD : 2 * HD] = k_ref[:, cols]
        out_ref[g, :, 2 * HD : 3 * HD] = v_ref[:, cols]


def pack(c, q, k, v, weight):
    depth, width = weight.shape
    steps = 2
    tokens = pl.BlockSpec((TOK, HEADS * HD // steps), lambda i, c_ref: (0, i))
    return pl.pallas_call(
        pack_kernel,
        out_shape=(
            jax.ShapeDtypeStruct((HEADS, TOK, 3 * HD), BF16),
            jax.ShapeDtypeStruct((depth, width // 2), BF16),
        ),
        grid_spec=pltpu.PrefetchScalarGridSpec(
            num_scalar_prefetch=1,
            grid=(steps,),
            in_specs=[tokens] * 3
            + [pl.BlockSpec((depth // steps, width // 2), lambda i, c_ref: (i, c_ref[0]))],
            out_specs=(
                pl.BlockSpec((HEADS // steps, TOK, 3 * HD), lambda i, c_ref: (i, 0, 0)),
                pl.BlockSpec((depth // steps, width // 2), lambda i, c_ref: (i, 0)),
            ),
        ),
    )(c, q, k, v, weight)


def attend_kernel(q_ref, kv0_ref, kv1_ref, out_ref):
    scale = math.log2(math.e) / math.sqrt(HD)
    half = kv0_ref.shape[0]
    token = lax.broadcasted_iota(jnp.int32, (2 * TOK, HD), 0)
    lane = lax.broadcasted_iota(jnp.int32, (2 * TOK, HD), 1)
    base = lane - lax.rem(token, 6) * 3
    row = lax.broadcasted_iota(jnp.int32, (8, 2 * TOK), 0)
    spot = lax.broadcasted_iota(jnp.int32, (8, 2 * TOK), 1)
    pick = jnp.where(lax.div(spot, 6) == row, 1.0, 0.0).astype(BF16)
    runs = [(ref, slice(at, at + KEYS)) for ref in (kv0_ref, kv1_ref) for at in range(0, half, KEYS)]

    def column(i, carry):
        q = q_ref[i]

        def scores(n):
            ref, rows = runs[n]
            return dot(q, ref[rows, 0:HD], ((1,), (1,)))

        ahead = scores(0)
        top = total = o = None
        for n, (ref, rows) in enumerate(runs):
            s = ahead
            if n + 1 < len(runs):
                ahead = scores(n + 1)
            high = jnp.max(s, axis=1, keepdims=True) * scale
            if n:
                before = top
                top = jnp.maximum(before, high)
                shrink = jnp.exp2(before - top)
            else:
                top = high
            p = jnp.exp2(s * scale - top)
            here = jnp.sum(p, axis=1, keepdims=True)
            part = dot(p.astype(BF16), ref[rows, HD : 2 * HD], ((1,), (0,)))
            total = total * shrink + here if n else here
            o = o * shrink + part if n else part
        o = (o / total).reshape(2, 8, TOK, HD)
        log = top + jnp.log2(total)
        hi = log.astype(BF16).astype(F32)
        mid = (log - hi).astype(BF16).astype(F32)
        lo = log - hi - mid
        hi, mid, lo = (x.reshape(2, 8, TOK, 1) for x in (hi, mid, lo))
        for z in range(8):
            piece = [jnp.concatenate([x[0, z], x[1, z]], axis=0) for x in (hi, mid, lo)]
            spread = jnp.where(
                base == 0,
                piece[0],
                jnp.where(base == 1, piece[1], jnp.where(base == 2, piece[2], 0.0)),
            )
            stats = dot(pick, spread.astype(BF16), ((1,), (0,)))
            out_ref[z, i] = jnp.concatenate([o[0, z], o[1, z], stats], axis=0).astype(BF16)
        return carry

    lax.fori_loop(0, 4, column, 0, unroll=2)


def attend(q, kvs):
    return pl.pallas_call(
        attend_kernel,
        out_shape=jax.ShapeDtypeStruct((8, 4, 56, HD), BF16),
        in_specs=[VMEM] * 3,
        out_specs=VMEM,
        compiler_params=pltpu.CompilerParams(vmem_limit_bytes=32 * MIB),
    )(q, *kvs)


def project_kernel(
    h_ref, c_ref, parts_ref, own_ref, other_ref, keep_ref, send_ref,
    near_ref, far_ref, att_ref, sum_ref, part_sems, far_sems,
):
    step = pl.program_id(0)
    block = sum_ref.shape[1]

    def far_copy(n):
        return pltpu.make_async_copy(
            other_ref.at[:, n * block : (n + 1) * block], far_ref.at[n], far_sems.at[n]
        )

    @pl.when(step == 0)
    def join():
        copies = [
            pltpu.make_async_copy(
                parts_ref.at[pl.ds(n * 4, 4)], near_ref.at[pl.ds(n * 4, 4)], part_sems.at[n]
            )
            for n in range(2)
        ]
        for copy in copies:
            copy.start()
        for n in range(2):
            far_copy(n).start()
        for n, copy in enumerate(copies):
            copy.wait()
            join_parts(near_ref, att_ref, range(n * 4, n * 4 + 4))

    @pl.when(step < 2)
    def near():
        sum_ref[...] = dot(att_ref[...], own_ref[...], ((1,), (0,)))

    for n in range(2):

        @pl.when(step == 2 + n)
        def far(n=n):
            far_copy(n).wait()
            sum_ref[...] = dot(att_ref[...], far_ref[n], ((1,), (0,)))

    h = h_ref[0]
    keep_ref[...] = sum_ref[pl.ds(pl.multiple_of(h * TOK, 8), TOK), :]
    send_ref[...] = sum_ref[pl.ds(pl.multiple_of((1 - h) * TOK, 8), TOK), :].astype(BF16)


def join_parts(parts_ref, att_ref, heads):
    token = lax.broadcasted_iota(jnp.int32, (2 * TOK, HD), 0)
    lane = lax.broadcasted_iota(jnp.int32, (2 * TOK, HD), 1)
    base = lane - lax.rem(token, 6) * 3
    mine = (base >= 0) & (base < 3)
    spot = lax.broadcasted_iota(jnp.int32, (2 * TOK, 8), 0)
    row = lax.broadcasted_iota(jnp.int32, (2 * TOK, 8), 1)
    pick = jnp.where(lax.div(spot, 6) == row, 1.0, 0.0).astype(BF16)
    for z in heads:
        logs = []
        pieces = [parts_ref[z, j].astype(F32) for j in range(4)]
        for j in range(4):
            spread = dot(pick, pieces[j][48:56].astype(BF16), ((1,), (0,)))
            logs.append(jnp.sum(jnp.where(mine, spread, 0.0), axis=1, keepdims=True))
        top = jnp.maximum(jnp.maximum(logs[0], logs[1]), jnp.maximum(logs[2], logs[3]))
        shares = [jnp.exp2(x - top) for x in logs]
        total = (shares[0] + shares[1]) + (shares[2] + shares[3])
        att = jnp.zeros((2 * TOK, HD), F32)
        for j in range(4):
            att = att + pieces[j][0:48] * (shares[j] / total)
        att_ref[:, z * HD : (z + 1) * HD] = att.astype(BF16)


def project(h, c, parts, own, other):
    depth, half = own.shape
    block = half // 2

    def place(i, h_ref, c_ref):
        side = jnp.where(i < 2, c_ref[0], 1 - c_ref[0])
        return 0, side * 2 + lax.rem(i, 2)

    return pl.pallas_call(
        project_kernel,
        out_shape=(
            jax.ShapeDtypeStruct((TOK, 2 * half), F32),
            jax.ShapeDtypeStruct((TOK, 2 * half), BF16),
        ),
        grid_spec=pltpu.PrefetchScalarGridSpec(
            num_scalar_prefetch=2,
            grid=(4,),
            in_specs=[
                pl.BlockSpec(memory_space=pl.ANY),
                pl.BlockSpec((depth, block), lambda i, h_ref, c_ref: (0, jnp.minimum(i, 1))),
                pl.BlockSpec(memory_space=pl.ANY),
            ],
            out_specs=(pl.BlockSpec((TOK, block), place), pl.BlockSpec((TOK, block), place)),
            scratch_shapes=[
                pltpu.VMEM(parts.shape, BF16),
                pltpu.VMEM((2, depth, block), BF16),
                pltpu.VMEM((2 * TOK, depth), BF16),
                pltpu.VMEM((2 * TOK, block), F32),
                pltpu.SemaphoreType.DMA((2,)),
                pltpu.SemaphoreType.DMA((2,)),
            ],
        ),
        compiler_params=pltpu.CompilerParams(vmem_limit_bytes=24 * MIB),
    )(h, c, parts, own, other)


def norm_kernel(
    h_ref, keep_ref, recv_ref, res_ref, cached_ref, use_ref, gate_ref, shift_ref, scale_ref, fw_ref, fb_ref,
    stream_ref, out_ref,
):
    eye = lax.broadcasted_iota(jnp.int32, (TOK, TOK), 0) == lax.broadcasted_iota(
        jnp.int32, (TOK, TOK), 1
    )
    mixed = res_ref[...].astype(F32)
    for b in range(2):
        used = use_ref[b : b + 1, :].astype(F32)
        column = jnp.sum(jnp.where(eye, used, 0.0), axis=1, keepdims=True)
        mixed = mixed + column * cached_ref[b].astype(F32)
    projected = keep_ref[...] + recv_ref[1 - h_ref[0]].astype(F32)
    stream = (mixed + gate_ref[...] * projected).astype(BF16)
    stream_ref[...] = stream
    x = stream.astype(F32)
    center = jnp.mean(x, axis=1, keepdims=True)
    off = x - center
    spread = jnp.mean(off * off, axis=1, keepdims=True)
    modulated = off * lax.rsqrt(spread + 1e-6) * (1.0 + scale_ref[...]) + shift_ref[...]
    latent = dot(modulated.astype(BF16), fw_ref[...], ((1,), (1,))) + fb_ref[...]
    latent = latent.astype(BF16)
    source = lax.broadcasted_iota(jnp.int32, (64, 64), 0)
    target = lax.broadcasted_iota(jnp.int32, (64, 64), 1)
    group = lax.div(target, 16)
    wanted = (lax.rem(group, 2) * 2 + lax.div(group, 2)) * 16 + lax.rem(target, 16)
    latent = dot(latent, jnp.where(source == wanted, 1.0, 0.0).astype(BF16), ((1,), (0,)))
    latent = latent.astype(BF16)
    band = lax.broadcasted_iota(jnp.int32, (FRAMES, TOK), 0)
    source = lax.broadcasted_iota(jnp.int32, (FRAMES, TOK), 1)
    first = lax.div(3 * band, 2) - 1
    pieces = [
        dot(jnp.where(source == first + k, 1.0, 0.0).astype(BF16), latent, ((1,), (0,)))
        for k in range(4)
    ]
    window = [x[:, 0:32] for x in pieces] + [x[:, 32:64] for x in pieces]
    window = jnp.concatenate(window, axis=1).reshape(FRAMES, 1, 2, HD)
    out_ref[...] = jnp.broadcast_to(window, (FRAMES, 32, 2, HD)).astype(BF16)


def norm(h, keep, recv, res, cached, use, gate, shift, scale, fw, fb):
    return pl.pallas_call(
        norm_kernel,
        out_shape=(
            jax.ShapeDtypeStruct(res.shape, BF16),
            jax.ShapeDtypeStruct((FRAMES, 32, 2, HD), BF16),
        ),
        in_specs=[SMEM] + [VMEM] * 10,
        out_specs=(VMEM, VMEM),
        compiler_params=pltpu.CompilerParams(vmem_limit_bytes=32 * MIB),
    )(h, keep, recv, res, cached, use, gate, shift, scale, fw, fb)


def frames_back(x, count, lane):
    if count == 0:
        return x
    moved = pltpu.roll(x, 64 * count, 1)
    start = x[:, 0:128]
    start = jnp.where(lane[:, 0:128] < 64, start, pltpu.roll(start, 64, 1))
    width = 128
    head = jnp.where(lane[:, 0:width] < 64 * count, start, moved[:, 0:width])
    return jnp.concatenate([head, moved[:, width:]], axis=1)


def column_shift(x, by, place):
    if by == 0:
        return x
    moved = pltpu.roll(x, (-by) % PIX, 1)
    edge = 63 if by == 1 else 0
    return jnp.where(place == edge, 0.0, moved)


def ready_kernel(w1_ref, w2_ref, out_ref):
    taps = w2_ref.shape[0]
    out_ref[0:taps, :] = w2_ref[...]
    out_ref[taps:, 0:taps] = jnp.transpose(w1_ref[...].astype(F32)).astype(BF16)


def ready(w1, w2):
    return pl.pallas_call(
        ready_kernel,
        out_shape=jax.ShapeDtypeStruct((432 + 512, 512), BF16),
        in_specs=[VMEM] * 2,
        out_specs=VMEM,
        cost_estimate=pl.CostEstimate(flops=0, bytes_accessed=1 << 23, transcendentals=0),
        compiler_params=pltpu.CompilerParams(vmem_limit_bytes=8 * MIB),
    )(w1, w2)


def conv_kernel(band_ref, own_ref, lat_ref, weights_ref, b1_ref, out_ref, taps_ref, first_ref, acc_ref):
    band = band_ref[0]
    lanes = own_ref[0]
    bias = jnp.transpose(jnp.broadcast_to(b1_ref[...], (8, 512)))[:, 0:1]
    lane16 = lax.broadcasted_iota(jnp.int32, (16, PIX), 1)
    place16 = lax.rem(lane16, 64)
    latent = jnp.transpose(lat_ref[...].astype(F32).reshape(PIX, 128))
    latent = jnp.where(lax.rem(band, 2) == 1, latent[16:128], latent[0:112])
    for r in range(7):
        row = latent[r * 16 : r * 16 + 16]
        for b in range(3):
            moved = column_shift(row, b - 1, place16)
            for t in range(3):
                at = r * 48 + b * 16
                taps_ref[t, at : at + 16, :] = frames_back(moved, 2 - t, lane16).astype(BF16)
    for r in range(5):
        patches = jnp.concatenate([taps_ref[t, r * 48 : r * 48 + 144, :] for t in range(3)], axis=0)
        first = dot(weights_ref[432:, 0:432], patches, ((1,), (0,))) + bias
        height = 3 * band - 1 + r
        inside = jnp.where((height >= 0) & (height < 48), 1.0, 0.0)
        rounded = (first * inside).astype(BF16)
        v = rounded.astype(F32)
        if 1 <= r <= 3:
            first_ref[r - 1] = rounded
        half = 0.5 * v
        act = (half * jnp.tanh(half) + half).astype(BF16)
        low, high = max(r - 2, 0), min(r, 2)
        z = dot(weights_ref[low * 144 : (high + 1) * 144, :], act, ((1,), (0,)))
        for a in range(low, high + 1):
            for t in range(3):
                at = ((a - low) * 3 + t) * 48
                if a == 0:
                    acc_ref[r - a, t] = z[at : at + 48]
                else:
                    acc_ref[r - a, t] += z[at : at + 48]
    for o in range(3):
        own = pl.ds(pl.multiple_of(lanes * 16, 16), 16)
        total = first_ref[o, own, :].astype(F32)
        for t in range(3):
            u = acc_ref[o, t, 16:32, :]
            u = u + column_shift(acc_ref[o, t, 0:16, :], -1, place16)
            u = u + column_shift(acc_ref[o, t, 32:48, :], 1, place16)
            u = frames_back(u, 2 - t, lane16)
            total = total + u
        out_ref[o] = total.astype(BF16)


def conv(band, own, lat, weights, b1):
    return pl.pallas_call(
        conv_kernel,
        out_shape=jax.ShapeDtypeStruct((3, 16, PIX), BF16),
        in_specs=[SMEM] * 2 + [VMEM] * 3,
        out_specs=VMEM,
        scratch_shapes=[
            pltpu.VMEM((3, 7 * 48, PIX), BF16),
            pltpu.VMEM((3, 512, PIX), BF16),
            pltpu.VMEM((3, 3, 48, PIX), F32),
        ],
        compiler_params=pltpu.CompilerParams(vmem_limit_bytes=28 * MIB),
    )(band, own, lat, weights, b1)


def per_device(
    residual_in,
    cached,
    use_cached,
    queries,
    attn_keys,
    values,
    gate_mod,
    shift_mod,
    scale_mod,
    out_weight,
    final_weight,
    final_bias,
    first_weight,
    first_bias,
    second_weight,
):
    model_width = residual_in.shape[-1]
    channels = first_weight.shape[-1]
    h = lax.axis_index("h").astype(jnp.int32).reshape(1)
    c = lax.axis_index("c").astype(jnp.int32).reshape(1)
    tokens = (x.reshape(TOK, HEADS * HD) for x in (queries, attn_keys, values))
    packed, mine = pack(c, *tokens, out_weight)
    mine = lax.all_gather(mine, "z", axis=0, tiled=True)
    moved = lax.all_to_all(packed, GRP, split_axis=0, concat_axis=0, tiled=True)
    moved = moved.reshape(FRAMES * TOK, 3 * HD)
    kv = jnp.broadcast_to(moved[None, :, HD:], (4, FRAMES * TOK, 2 * HD))
    kv = lax.all_to_all(kv, "ya", split_axis=0, concat_axis=0, tiled=True)
    kv = kv.reshape(4 * FRAMES * TOK, 2 * HD)
    kvs = [kv, lax.ppermute(kv, "c", [(0, 1), (1, 0)])]
    q = jnp.broadcast_to(moved[None, :, :HD], (4, FRAMES * TOK, HD))
    q = lax.all_to_all(q, ("yb", "l"), split_axis=0, concat_axis=0, tiled=True)
    parts = attend(q, kvs)
    parts, mine = lax.optimization_barrier((parts, mine))
    theirs = lax.ppermute(mine, "c", [(0, 1), (1, 0)])
    one = jnp.where(c[0] >= 0, 1.0, 0.0).astype(BF16)
    mine = mine * one
    parts = lax.all_to_all(
        parts.reshape(32, 56, HD), ("z", "yb", "l"), split_axis=0, concat_axis=0, tiled=True
    )
    keep, send = project(h, c, parts.reshape(8, 4, 56, HD), mine, theirs)
    recv = lax.all_gather(send, "h", axis=0)
    stream, windows = norm(
        h,
        keep,
        recv,
        residual_in.reshape(TOK, model_width),
        cached.reshape(2, TOK, model_width),
        use_cached.reshape(2, TOK),
        gate_mod[None, :],
        shift_mod[None, :],
        scale_mod[None, :],
        final_weight.T,
        final_bias[None, :],
    )
    windows, w1, w2 = lax.optimization_barrier((windows, first_weight, second_weight))
    lat = lax.all_to_all(
        windows.reshape(512, 2, HD), GRP + COL, split_axis=0, concat_axis=0, tiled=True
    )
    band = lax.axis_index(GRP).astype(jnp.int32).reshape(1)
    own = lax.axis_index(COL).astype(jnp.int32).reshape(1)
    w2 = jnp.transpose(w2, (2, 1, 3, 0, 4)).reshape(27 * 16, channels)
    weights = ready(w1.reshape(27 * 16, channels), w2)
    out = conv(band, own, lat, weights, first_bias[None, :])
    return stream.reshape(residual_in.shape), jnp.transpose(out, (1, 0, 2))


def solution(mesh):
    fine = Mesh(mesh.devices.reshape(2, 8, 4, 2, 2, 2), GRP + COL)
    return jax.shard_map(
        per_device,
        mesh=fine,
        in_specs=(
            P(GRP, COL, None, None),
            P(None, GRP, COL, None, None),
            P(None, GRP, COL, None),
            P(GRP, COL, None, None),
            P(GRP, COL, None, None),
            P(GRP, COL, None, None),
            P(),
            P(),
            P(),
            P(GRP, None),
            P(),
            P(),
            P(),
            P(),
            P(COL, None, None, None, None),
        ),
        out_specs=(P(GRP, COL, None, None), P(COL, GRP, None)),
        check_vma=False,
    )
```
